256 devices in a mesh: space: 16 (over y_lo, x, core), tm: 16 (over z, y_hi).
Axes of the slice: x: 4, y: 4 (y_hi: 2, y_lo: 2; y = y_hi * 2 + y_lo), z: 8, core: 2. Of those that a mesh axis runs over, the one named last changes fastest.
Arguments:
- record: float32 [3072, 65536], P('tm', 'space'), may hold values from -40 to 40
- mode_basis: float32 [21, 48, 48], replicated, may hold values from -0.2 to 1.2
- slow_picks: int32 [21, 32], replicated, may hold values from 0 to 47, all different within a row
- phases: int32 [21], replicated, may hold values from 0 to 3
Outputs:
- residual_record: float32 [3072, 65536], P('tm', 'space')
The draws below stay inside these ranges and needn't reach their ends.
Inputs may be any that keep to these rules, and one draw needn't show every extreme that they name: `slow_picks`: the 32 entries of a row are different.
All inputs are finite; a program needn't handle non-finite values.
Results may differ from the reference program's by a relative error of at most 0.003.
Values may be sent and summed in bfloat16 or wider, within the bound.
A program may use at most 64 MiB of HBM per device.

```python
import jax
import jax.numpy as jnp
from jax import lax

M = 48
R = 32
WINDOWS = 21
POINTS = 65536
TIMES = 3072


def draw_record(key, part):
    key = jax.random.fold_in(key, 11)
    key_main, key_point, key_snap = jax.random.split(key, 3)
    point_scale = jnp.exp(jax.random.uniform(key_point, (1, POINTS), jnp.float32, jnp.log(0.3), jnp.log(3.0)))
    snap_scale = jnp.exp(jax.random.uniform(key_snap, (TIMES, 1), jnp.float32, jnp.log(0.5), jnp.log(2.0)))
    values = jax.random.truncated_normal(key_main, -5.0, 5.0, (TIMES, POINTS), jnp.float32)
    return values * snap_scale * point_scale


def draw_mode_basis(key, part):
    key = jax.random.fold_in(key, 23)
    noise = 0.06 * jax.random.truncated_normal(key, -3.0, 3.0, (WINDOWS, M, M), jnp.float32)
    return noise + jnp.eye(M, dtype=jnp.float32)[None]


def set_ends(drawn, key, low, top_value):
    index_at = [jax.random.randint(jax.random.fold_in(key, axis), (), 0, length) for axis, length in enumerate(drawn.shape)]
    widest = drawn.shape.index(max(drawn.shape))
    next_to = index_at[:widest] + [(index_at[widest] + 1) % drawn.shape[widest]] + index_at[widest + 1:]
    return drawn.at[tuple(index_at)].set(low).at[tuple(next_to)].set(top_value)


def picks_of(stream_key, rows, count, top, lift):
    sequence = jax.random.permutation(jax.random.fold_in(stream_key, 1), count)
    boost = sequence
    for power in range(3):
        boost = boost * boost // count
    boost = boost * lift // count
    tickets = jax.random.randint(jax.random.fold_in(stream_key, 2), (rows, count), 0, 4096) + boost
    sure = jax.random.permutation(jax.random.fold_in(stream_key, 3), rows)[jnp.arange(count) % rows]
    tickets = jnp.where(jnp.arange(rows)[:, None] == sure[None, :], 1 << 14, tickets)
    score = tickets * count + jnp.arange(count)
    return lax.top_k(score.astype(jnp.int32), top)[1].astype(jnp.int32)


def setup_inputs(seed: int = 0) -> dict:
    keys = jax.random.split(jax.random.key(seed), 5)
    record = draw_record(jax.random.fold_in(keys[4], 71), 0)
    mode_basis = draw_mode_basis(jax.random.fold_in(keys[4], 71), 0)
    slow_picks = picks_of(keys[2], WINDOWS, M, R, 0)
    phases = set_ends(jax.random.randint(keys[3], (WINDOWS,), 0, 4), jax.random.fold_in(keys[3], 1), 0, 3).astype(jnp.int32)
    return dict(record=record, mode_basis=mode_basis, slow_picks=slow_picks, phases=phases)


precise = lax.Precision.HIGHEST

def choose_columns(basis_w, picks_w, gram, points):
    size_m = basis_w.shape[1]
    modes_r = picks_w.shape[1]
    onehot = (picks_w[:, :, None] == jnp.arange(size_m, dtype=jnp.int32)[None, None, :]).astype(jnp.float32)
    chosen = jnp.einsum('wmn,wrn->wmr', basis_w, onehot, precision=precise)
    inner = jnp.einsum('wmn,wnr->wmr', gram, chosen, precision=precise)
    kernel = jnp.einsum('wmr,wms->wrs', chosen, inner, precision=precise) + 1e-05 * jnp.eye(modes_r, dtype=jnp.float32)[None]
    factor = jnp.linalg.cholesky(kernel)
    solved = lax.linalg.triangular_solve(factor, chosen, left_side=False, lower=True, transpose_a=True)
    return solved / jnp.sqrt(jnp.asarray(points, jnp.float32))

def reference(record, mode_basis, slow_picks, phases):
    field = record
    offset_base = 0
    for level in range(3):
        window_count = 4 ** level
        span_len = TIMES // window_count
        stride = span_len // M
        offsets = phases[offset_base:offset_base + window_count] % stride
        indices = (jnp.arange(window_count, dtype=jnp.int32) * span_len)[:, None] + offsets[:, None] + stride * jnp.arange(M, dtype=jnp.int32)[None, :]
        samples = field[indices.reshape(-1)].astype(jnp.bfloat16).reshape(window_count, M, POINTS)
        widened = samples.astype(jnp.float32)
        gram = jnp.einsum('wmp,wnp->wmn', widened, widened, precision=precise) / POINTS
        weights = choose_columns(mode_basis[offset_base:offset_base + window_count], slow_picks[offset_base:offset_base + window_count], gram, POINTS)
        modes = jnp.einsum('wmr,wmp->wrp', weights, widened, precision=precise)
        segments = field.reshape(window_count, span_len, POINTS)
        amplitude = jnp.einsum('wrp,wtp->wrt', modes, segments, precision=precise)
        slow = jnp.einsum('wrt,wrp->wtp', amplitude, modes, precision=precise)
        field = (segments - slow).reshape(TIMES, POINTS)
        offset_base = offset_base + window_count
    return field
```

```python
import functools

import jax
import jax.numpy as jnp
from jax import lax
from jax.experimental import pallas as pl
from jax.experimental.pallas import tpu as pltpu
from jax.sharding import PartitionSpec as P

M = 48
R = 32
LEVELS = 3
SEG = 128
WIDTH = 512
EPS = 1e-5
MESH = pl.DeviceIdType.MESH
EXACT = lax.Precision.HIGHEST
VMEM_LIMIT = 56 * 1024 * 1024


def dot_nt(a, b):
    return lax.dot_general(a, b, (((1,), (1,)), ((), ())), preferred_element_type=jnp.float32)


def exact(a, b):
    return jnp.dot(a, b, precision=EXACT, preferred_element_type=jnp.float32)


def collect(
    nt, ns, owners,
    phases, picks, basis_hbm, record,
    y_out, sums_out, chosen_out,
    field, split, y, outbox, got0, got1, wide, basis, chosen, cross, own_gram, part, inbox, total,
    load_sem, basis_sem, send0_sem, recv0_sem, send1_sem, recv1_sem, sendr_sem, recvr_sem, senda_sem, recva_sem,
):
    steps, points = record.shape
    segs = points // SEG
    me_t = lax.axis_index("tm")
    me_s = lax.axis_index("space")
    group = nt // 4
    first = me_t // group * group
    rows0 = M // nt
    rows1 = M // group
    span = LEVELS * R // owners

    loads = [
        pltpu.make_async_copy(
            record.at[:, j * SEG : (j + 1) * SEG], field.at[pl.ds(j * steps, steps)], load_sem.at[j]
        )
        for j in range(segs)
    ]
    for load in loads:
        load.start()
    q1 = 1 + me_t // group
    q2 = 5 + me_t
    fetches = [
        pltpu.make_async_copy(basis_hbm.at[q], basis.at[level], basis_sem.at[level])
        for level, q in enumerate((0, q1, q2))
    ]
    for fetch in fetches:
        fetch.start()

    barrier = pltpu.get_barrier_semaphore()
    for d in range(1, nt):
        pl.semaphore_signal(barrier, inc=1, device_id={"tm": lax.rem(me_t + d, nt)}, device_id_type=MESH)
    for d in range(1, ns):
        pl.semaphore_signal(barrier, inc=1, device_id={"space": lax.rem(me_s + d, ns)}, device_id_type=MESH)

    for load in loads:
        load.wait()
    off0 = lax.rem(phases[0], steps * nt // M)
    off1 = lax.rem(phases[q1], steps * group // M)
    off2 = lax.rem(phases[q2], steps // M)
    stride0 = steps * nt // M
    stride1 = steps * group // M
    stride2 = steps // M

    for r in range(rows0):
        outbox[r * segs : (r + 1) * segs] = field[pl.ds(off0 + stride0 * r, segs, stride=steps), :].astype(
            jnp.bfloat16
        )
    for r in range(rows0, rows0 + rows1):
        outbox[r * segs : (r + 1) * segs] = field[
            pl.ds(off1 + stride1 * (r - rows0), segs, stride=steps), :
        ].astype(jnp.bfloat16)
    got0[me_t] = outbox[: rows0 * segs]
    got1[me_t - first] = outbox[rows0 * segs :]

    pl.semaphore_wait(barrier, nt - 1 + ns - 1)

    sends = []
    for d in range(1, group):
        tgt = first + lax.rem(me_t - first + d, group)
        sends.append(
            pltpu.make_async_remote_copy(
                src_ref=outbox.at[pl.ds(rows0 * segs, rows1 * segs)], dst_ref=got1.at[me_t - first],
                send_sem=send1_sem.at[d], recv_sem=recv1_sem.at[me_t - first],
                device_id={"tm": tgt}, device_id_type=MESH,
            )
        )
    for d in range(1, nt):
        tgt = lax.rem(me_t + d, nt)
        sends.append(
            pltpu.make_async_remote_copy(
                src_ref=outbox.at[pl.ds(0, rows0 * segs)], dst_ref=got0.at[me_t],
                send_sem=send0_sem.at[d], recv_sem=recv0_sem.at[me_t],
                device_id={"tm": tgt}, device_id_type=MESH,
            )
        )
    for copy in sends:
        copy.start()

    def part_columns(c, carry):
        cols = pl.ds(pl.multiple_of(c * SEG, SEG), SEG)
        block = field[pl.ds(pl.multiple_of(c * steps, steps), steps), :]
        high = block.astype(jnp.bfloat16)
        split[:steps, cols] = high
        split[steps:, cols] = (block - high.astype(jnp.float32)).astype(jnp.bfloat16)
        x2 = field[pl.ds(c * steps + off2, M, stride=stride2), :]
        high2 = x2.astype(jnp.bfloat16)
        y[2 * M : 3 * M, cols] = high2
        y[3 * M :, cols] = (x2 - high2.astype(jnp.float32)).astype(jnp.bfloat16)
        return carry

    lax.fori_loop(0, segs, part_columns, 0)

    for fetch in fetches:
        fetch.wait()
    lanes = lax.broadcasted_iota(jnp.int32, (M, LEVELS * R), 1)
    rows_m = lax.broadcasted_iota(jnp.int32, (M, LEVELS * R), 0)
    p012 = jnp.concatenate([picks[pl.ds(q, 1), :] for q in (0, q1, q2)], axis=1)
    for level in range(LEVELS):
        hit = (rows_m == p012) & (lanes >= R * level) & (lanes < R * (level + 1))
        chosen[M * level : M * (level + 1)] = exact(basis[level], hit.astype(jnp.float32))
    chosen[LEVELS * M :] = chosen[(LEVELS - 1) * M : LEVELS * M]

    for d in range(1, group):
        src = lax.rem(me_t - first + d, group)
        pltpu.make_async_remote_copy(
            src_ref=outbox.at[pl.ds(rows0 * segs, rows1 * segs)], dst_ref=got1.at[src],
            send_sem=send1_sem.at[d], recv_sem=recv1_sem.at[src],
            device_id={"tm": first + src}, device_id_type=MESH,
        ).wait_recv()
    wide[...] = got1[...].reshape(M * segs, SEG).astype(jnp.float32)
    for j in range(segs):
        y[M : 2 * M, j * SEG : (j + 1) * SEG] = wide[pl.ds(j, M, stride=segs), :].astype(jnp.bfloat16)
    for d in range(1, nt):
        src = lax.rem(me_t + d, nt)
        pltpu.make_async_remote_copy(
            src_ref=outbox.at[pl.ds(0, rows0 * segs)], dst_ref=got0.at[src],
            send_sem=send0_sem.at[d], recv_sem=recv0_sem.at[src],
            device_id={"tm": src}, device_id_type=MESH,
        ).wait_recv()
    wide[...] = got0[...].reshape(M * segs, SEG).astype(jnp.float32)
    for j in range(segs):
        y[:M, j * SEG : (j + 1) * SEG] = wide[pl.ds(j, M, stride=segs), :].astype(jnp.bfloat16)

    cross[...] = jnp.zeros_like(cross)
    own_gram[...] = jnp.zeros_like(own_gram)

    def products(c, carry):
        cols = pl.ds(pl.multiple_of(c * WIDTH, WIDTH), WIDTH)
        rows = y[:, cols]
        cross[...] += dot_nt(rows, split[:steps, cols]) + dot_nt(rows, split[steps:, cols])
        own_gram[...] += dot_nt(rows, rows)
        return carry

    lax.fori_loop(0, points // WIDTH, products, 0)
    turned = chosen[...].T
    part[:, 256:] = jnp.zeros_like(part[:, 256:])
    part[:, 192:256] = jnp.zeros_like(part[:, 192:256])
    part[:, :steps] = exact(turned, cross[...])
    part[:, 256 : 256 + LEVELS * R] = exact(exact(turned, own_gram[...]), chosen[...])

    sums = []
    for d in range(1, ns):
        tgt = lax.rem(me_s + d, ns)
        safe = lax.rem(tgt, owners)
        copy = pltpu.make_async_remote_copy(
            src_ref=part.at[pl.ds(pl.multiple_of(safe * span, span), span)], dst_ref=inbox.at[me_s],
            send_sem=sendr_sem.at[d], recv_sem=recvr_sem.at[me_s],
            device_id={"space": tgt}, device_id_type=MESH,
        )
        sums.append((tgt, copy))
        pl.when(tgt < owners)(copy.start)

    mine = pl.ds(pl.multiple_of(lax.rem(me_s, owners) * span, span), span)
    hands = [
        pltpu.make_async_remote_copy(
            src_ref=total.at[mine], dst_ref=total.at[mine],
            send_sem=senda_sem.at[d], recv_sem=recva_sem.at[me_s],
            device_id={"space": lax.rem(me_s + d, ns)}, device_id_type=MESH,
        )
        for d in range(1, ns)
    ]

    @pl.when(me_s < owners)
    def _():
        acc = part[mine, :]
        for d in range(1, ns):
            src = lax.rem(me_s + d, ns)
            pltpu.make_async_remote_copy(
                src_ref=part.at[mine], dst_ref=inbox.at[src],
                send_sem=sendr_sem.at[d], recv_sem=recvr_sem.at[src],
                device_id={"space": src}, device_id_type=MESH,
            ).wait_recv()
            acc = acc + inbox[src]
        total[mine, :] = acc
        for hand in hands:
            hand.start()

    y_out[...] = y[...]
    chosen_out[...] = chosen[...]

    for d in range(1, ns):
        src = lax.rem(me_s + d, ns)
        theirs = pl.ds(pl.multiple_of(lax.rem(src, owners) * span, span), span)
        arrival = pltpu.make_async_remote_copy(
            src_ref=total.at[mine], dst_ref=total.at[theirs],
            send_sem=senda_sem.at[d], recv_sem=recva_sem.at[src],
            device_id={"space": src}, device_id_type=MESH,
        )
        pl.when(src < owners)(arrival.wait_recv)
    sums_out[...] = total[...]

    for copy in sends:
        copy.wait_send()
    for tgt, copy in sums:
        pl.when(tgt < owners)(copy.wait_send)

    @pl.when(me_s < owners)
    def _():
        for hand in hands:
            hand.wait_send()


def eliminate(block, pivot_lane):
    parts = [block[8 * g : 8 * (g + 1)] for g in range(R // 8)]
    sub = lax.broadcasted_iota(jnp.int32, parts[0].shape, 0)
    for k in range(R):
        g, i = divmod(k, 8)
        lane = pivot_lane + k
        pivot_row = parts[g][i : i + 1, :] / parts[g][i : i + 1, lane : lane + 1]
        fresh = []
        for h in range(R // 8):
            moved = parts[h] - parts[h][:, lane : lane + 1] * pivot_row
            fresh.append(jnp.where(sub == i, pivot_row, moved) if h == g else moved)
        parts = fresh
    return jnp.concatenate(parts, axis=0)


def update(points_all, sums, chosen, y, record, out_hbm, field, out, weights, load_sem, store_sem):
    steps, points = record.shape
    load = pltpu.make_async_copy(record, field, load_sem)
    load.start()
    blocks = [sums[R * level : R * (level + 1), :] / points_all for level in range(LEVELS)]
    lane = lax.broadcasted_iota(jnp.int32, blocks[0].shape, 1)
    row = lax.broadcasted_iota(jnp.int32, blocks[0].shape, 0)
    unit = (lane == steps + row).astype(jnp.float32)
    solved = []
    for level in range(LEVELS):
        at = 256 + R * level
        block = blocks[level]
        ridge = jnp.where(lane == at + row, block + EPS, block) + unit
        done = eliminate(ridge, at)
        inverse = done[:, steps : steps + R]
        done = jnp.where((lane >= at) & (lane < at + R), exact(inverse, block), done)
        solved.append(done)
        if level < LEVELS - 1:
            twice = done + EPS * exact(inverse, done)
            for later in range(level + 1, LEVELS):
                blocks[later] = blocks[later] - exact(blocks[later][:, at : at + R], twice)
                blocks[later] = jnp.where((lane >= steps) & (lane < 256), 0.0, blocks[later])
    j2 = solved[2][:, :steps]
    j1 = solved[1][:, :steps] - exact(solved[1][:, 256 + 2 * R : 256 + 3 * R], j2)
    j0 = (
        solved[0][:, :steps]
        - exact(solved[0][:, 256 + 2 * R : 256 + 3 * R], j2)
        - exact(solved[0][:, 256 + R : 256 + 2 * R], j1)
    )
    turned = exact(chosen[...], jnp.concatenate([j0, j1, j2], axis=0)).T
    high = turned.astype(jnp.bfloat16)
    weights[:steps] = high
    weights[steps:] = (turned - high.astype(jnp.float32)).astype(jnp.bfloat16)
    load.wait()
    stores = []
    for c in range(points // WIDTH):
        cols = slice(c * WIDTH, (c + 1) * WIDTH)
        slow = jnp.dot(weights[...], y[:, cols], preferred_element_type=jnp.float32)
        out[:, cols] = field[:, cols] - (slow[:steps] + slow[steps:])
        store = pltpu.make_async_copy(out.at[:, cols], out_hbm.at[:, cols], store_sem.at[c])
        store.start()
        stores.append(store)
    for store in stores:
        store.wait()


def body(nt, ns, record, mode_basis, slow_picks, phases):
    steps, points = record.shape
    segs = points // SEG
    owners = max(o for o in (1, 2, 4, 6, 12) if o <= ns)
    group = nt // 4
    dma = pltpu.SemaphoreType.DMA
    vmem = pl.BlockSpec(memory_space=pltpu.VMEM)
    hbm = pl.BlockSpec(memory_space=pl.ANY)
    y, sums, chosen = pl.pallas_call(
        functools.partial(collect, nt, ns, owners),
        out_shape=[
            jax.ShapeDtypeStruct((4 * M, points), jnp.bfloat16),
            jax.ShapeDtypeStruct((LEVELS * R, 384), jnp.float32),
            jax.ShapeDtypeStruct((4 * M, LEVELS * R), jnp.float32),
        ],
        in_specs=[pl.BlockSpec(memory_space=pltpu.SMEM), vmem, hbm, hbm],
        out_specs=[vmem, vmem, vmem],
        scratch_shapes=[
            pltpu.VMEM((segs * steps, SEG), jnp.float32),
            pltpu.VMEM((2 * steps, points), jnp.bfloat16),
            pltpu.VMEM((4 * M, points), jnp.bfloat16),
            pltpu.VMEM(((M // nt + M // group) * segs, SEG), jnp.bfloat16),
            pltpu.VMEM((nt, M // nt * segs, SEG), jnp.bfloat16),
            pltpu.VMEM((group, M // group * segs, SEG), jnp.bfloat16),
            pltpu.VMEM((M * segs, SEG), jnp.float32),
            pltpu.VMEM((LEVELS, M, M), jnp.float32),
            pltpu.VMEM((4 * M, LEVELS * R), jnp.float32),
            pltpu.VMEM((4 * M, steps), jnp.float32),
            pltpu.VMEM((4 * M, 4 * M), jnp.float32),
            pltpu.VMEM((LEVELS * R, 384), jnp.float32),
            pltpu.VMEM((ns, LEVELS * R // owners, 384), jnp.float32),
            pltpu.VMEM((LEVELS * R, 384), jnp.float32),
            dma((segs,)), dma((LEVELS,)),
            dma((nt,)), dma((nt,)), dma((group,)), dma((group,)),
            dma((ns,)), dma((ns,)), dma((ns,)), dma((ns,)),
        ],
        compiler_params=pltpu.CompilerParams(
            collective_id=0, has_side_effects=True, vmem_limit_bytes=VMEM_LIMIT
        ),
        name="collect",
    )(phases, slow_picks, mode_basis, record)
    return pl.pallas_call(
        functools.partial(update, float(points * ns)),
        out_shape=jax.ShapeDtypeStruct((steps, points), jnp.float32),
        in_specs=[vmem, vmem, vmem, hbm],
        out_specs=hbm,
        scratch_shapes=[
            pltpu.VMEM((steps, points), jnp.float32),
            pltpu.VMEM((steps, points), jnp.float32),
            pltpu.VMEM((2 * steps, 4 * M), jnp.bfloat16),
            dma(()), dma((points // WIDTH,)),
        ],
        compiler_params=pltpu.CompilerParams(vmem_limit_bytes=VMEM_LIMIT),
        name="update",
    )(sums, chosen, y, record)


def solution(mesh):
    in_specs = (P("tm", "space"), P(), P(), P())
    out_specs = P("tm", "space")
    return jax.shard_map(
        functools.partial(body, mesh.shape["tm"], mesh.shape["space"]),
        mesh=mesh, in_specs=in_specs, out_specs=out_specs, check_vma=False,
    )
```

```python
import jax
import jax.numpy as jnp
from jax import lax
from jax.experimental import pallas as pl
from jax.experimental.pallas import tpu as pltpu
from jax.sharding import PartitionSpec as P

M = 48
R = 32
LANES = 128
WIDTH = 512
EPS = 1e-5
AHEAD = 2
MESH = pl.DeviceIdType.MESH
EXACT = lax.Precision.HIGHEST
VMEM_LIMIT = 24 * 1024 * 1024
NT = 16
NS = 16
NZ = NT // 2
GROUP = 4
STEPS = 192
POINTS = 4096
SEGS = POINTS // LANES
TILES = STEPS // 8
BLOCK = SEGS * 8
ROWS0 = M // NT
ROWS1 = M // GROUP
X0 = STEPS
X1 = X0 + M
X2 = X1 + M
ALL = X2 + 2 * M
LANE1 = 64
LANE0 = 96
OWNERS2 = 8


def dot_nt(a, b):
    return lax.dot_general(a, b, (((1,), (1,)), ((), ())), preferred_element_type=jnp.float32)


def exact(a, b, dims=((1,), (0,))):
    return lax.dot_general(a, b, (dims, ((), ())), precision=EXACT, preferred_element_type=jnp.float32)


def collect(
    phases_hbm, picks_hbm, basis_hbm, record,
    rows, sums, chosen, among,
    phases, picks, field_even, field_odd, got0, got1, wide0, wide1, basis, turned, pad,
    part2, inbox2, total2, part01, inbox01, total01,
    load_sem, small_sem, recv0_sem, sem,
):
    send0_sem, sendy_sem, recvy_sem, send1_sem, recv1_sem = [sem.at[i] for i in range(5)]
    sems2, sems01 = [[sem.at[i] for i in range(j, j + 4)] for j in (5, 9)]
    me_t = lax.axis_index("tm")
    me_s = lax.axis_index("space")
    first = me_t // GROUP * GROUP

    barrier = pltpu.get_barrier_semaphore()
    for d in range(1, NT):
        pl.semaphore_signal(barrier, inc=1, device_id={"tm": lax.rem(me_t + d, NT)}, device_id_type=MESH)
    for d in range(1, NS):
        pl.semaphore_signal(barrier, inc=1, device_id={"space": lax.rem(me_s + d, NS)}, device_id_type=MESH)

    get_phases = pltpu.make_async_copy(phases_hbm, phases, small_sem.at[3])
    get_phases.start()
    load_even, load_odd = [
        pltpu.make_async_copy(record.at[:, i], half.reshape(TILES // 2, BLOCK, LANES), load_sem.at[i])
        for i, half in enumerate((field_even, field_odd))
    ]
    load_even.start()
    q1 = 1 + me_t // GROUP
    q2 = 5 + me_t
    fetches = [
        pltpu.make_async_copy(basis_hbm.at[q], basis.at[level], small_sem.at[level])
        for level, q in enumerate((0, q1, q2))
    ]
    fetches.append(pltpu.make_async_copy(picks_hbm, picks, small_sem.at[4]))
    for fetch in fetches:
        fetch.start()
    load_odd.start()

    get_phases.wait()
    off0 = lax.rem(phases[0], STEPS * NT // M)
    off1 = lax.rem(phases[q1], STEPS * GROUP // M)
    off2 = lax.rem(phases[q2], STEPS // M)
    load_even.wait()
    for r in range(ROWS0):
        start = r * (STEPS // ROWS0) // 16 * BLOCK
        got0[me_t, r * SEGS : (r + 1) * SEGS] = field_even[pl.ds(start + off0, SEGS, stride=8), :].astype(
            jnp.bfloat16
        )
    for r in range(ROWS1):
        start = r * (STEPS // ROWS1) // 16 * BLOCK
        got1[me_t - first, r * SEGS : (r + 1) * SEGS] = field_even[
            pl.ds(start + off1, SEGS, stride=8), :
        ].astype(jnp.bfloat16)

    pl.semaphore_wait(barrier, NT - 1 + NS - 1)

    z = me_t // 2
    h = lax.rem(me_t, 2)
    partner = me_t + 1 - 2 * h
    near = me_t + 2 - 4 * lax.rem(z, 2)
    across = near + 1 - 2 * h

    def along0(target, owner, send_sem, recv_sem):
        return pltpu.make_async_remote_copy(
            src_ref=got0.at[owner], dst_ref=got0.at[owner], send_sem=send_sem, recv_sem=recv_sem,
            device_id={"tm": target}, device_id_type=MESH,
        )

    def along1(target, owner):
        return pltpu.make_async_remote_copy(
            src_ref=got1.at[owner - first], dst_ref=got1.at[owner - first],
            send_sem=send1_sem, recv_sem=recv1_sem,
            device_id={"tm": target}, device_id_type=MESH,
        )

    def whole(ref, count, send_sem, recv_sem):
        place = ref.at[pl.ds(0, count)]
        return pltpu.make_async_remote_copy(
            src_ref=place, dst_ref=place, send_sem=send_sem, recv_sem=recv_sem,
            device_id={"tm": partner}, device_id_type=MESH,
        )

    hops = (1, -1, 2, -2, 3, -3, 4)
    turn = [lax.rem(z + d + NZ, NZ) for d in hops]
    out0 = [along0(2 * turn[i] + h, me_t, send0_sem, recv0_sem.at[z]) for i in range(7)]
    in0 = [along0(2 * turn[i] + h, 2 * turn[i] + h, send0_sem, recv0_sem.at[turn[i]]) for i in range(7)]
    over0 = [along0(partner, 2 * turn[i] + h, sendy_sem, recvy_sem) for i in range(7)]
    over0.append(along0(partner, me_t, sendy_sem, recvy_sem))
    peers1 = (near, partner, across)
    out1 = [along1(peer, me_t) for peer in peers1]
    for copy in (over0[7], *out0, *out1):
        copy.start()

    def widen(wide, got, slot):
        size = got.shape[1]
        wide[pl.ds(pl.multiple_of(slot * size, size), size)] = got[slot].astype(jnp.float32)

    def pass0(i):
        in0[i].wait_recv()
        over0[i].start()
        widen(wide0, got0, 2 * turn[i] + h)

    load_odd.wait()

    def part_columns(c, carry):
        cols = pl.ds(pl.multiple_of(c * LANES, LANES), LANES)
        at = pl.multiple_of(c * 8, 8)
        for p in range(TILES // 2):
            pair = jnp.concatenate(
                [field_even[pl.ds(p * BLOCK + at, 8), :], field_odd[pl.ds(p * BLOCK + at, 8), :]], axis=0
            )
            rows[16 * p : 16 * (p + 1), cols] = pair.astype(jnp.bfloat16)
        x2 = jnp.concatenate(
            [
                half[pl.ds(at + off2 + more, TILES // 2, stride=BLOCK), :]
                for half in (field_even, field_odd)
                for more in (0, 4)
            ],
            axis=0,
        )
        high2 = x2.astype(jnp.bfloat16)
        rows[X2 : X2 + M, cols] = high2
        rows[X2 + M :, cols] = (x2 - high2.astype(jnp.float32)).astype(jnp.bfloat16)
        return carry

    lax.fori_loop(0, SEGS // 2, part_columns, 0)
    widen(wide0, got0, me_t)
    widen(wide1, got1, me_t - first)
    pass0(0)
    pass0(1)
    lax.fori_loop(SEGS // 2, SEGS, part_columns, 0)
    pass0(2)
    pass0(3)

    for fetch in fetches:
        fetch.wait()
    none = lambda count: [jnp.full((1, R), -1, jnp.int32)] * count
    row_m = lax.broadcasted_iota(jnp.int32, (M, LANES), 0)
    for level, (q, place, at) in enumerate(((0, 3, 0), (q1, 2, M), (q2, 0, 2 * M))):
        spots = jnp.concatenate([*none(place), picks[pl.ds(q, 1), :], *none(3 - place)], axis=1)
        columns = exact(basis[level], (row_m == spots).astype(jnp.float32))
        if level == 2:
            pad[...] = columns
            columns = jnp.concatenate([pad[pl.ds(i, M // 4, stride=4), :] for i in range(4)], axis=0)
            chosen[3 * M :] = columns
        chosen[at : at + M] = columns
    turned[...] = chosen[...].T
    at_row = lax.broadcasted_iota(jnp.int32, (STEPS, M), 0)
    order = lax.broadcasted_iota(jnp.int32, (STEPS, M), 1)
    rank = lax.rem(order, M // 4) * 4 + order // (M // 4)
    among[...] = exact((at_row == 4 * rank + off2).astype(jnp.float32), chosen[2 * M : 3 * M])
    for i in range(4, 7):
        pass0(i)

    def put(ref, tiles):
        for g in range(tiles[0].shape[0] // 8):
            for t in range(2):
                ref[2 * g + t] = tiles[t][8 * g : 8 * (g + 1)]

    space = jnp.zeros((R, 2 * LANES - STEPS), jnp.float32)
    by_field2 = exact(turned[:R, 2 * M :], dot_nt(rows[:STEPS], rows[X2:]), ((1,), (1,)))
    put(part2, [by_field2[:, :LANES], jnp.concatenate([by_field2[:, LANES:], space], axis=1)])

    def others(owners, do):
        if owners == NS:
            do(NS - 1)
        else:
            pl.when(me_s < owners)(lambda: do(owners - 1))
            pl.when(me_s >= owners)(lambda: do(owners))

    def spread(part, inbox, sems, owners):
        for d in range(1, NS):
            tgt = lax.rem(me_s + d, NS)
            copy = pltpu.make_async_remote_copy(
                src_ref=part.at[lax.rem(tgt, owners)], dst_ref=inbox.at[me_s],
                send_sem=sems[0], recv_sem=sems[1],
                device_id={"space": tgt}, device_id_type=MESH,
            )
            if owners == NS:
                copy.start()
            else:
                pl.when(tgt < owners)(copy.start)

    def reduce(part, inbox, total, sems, owners):
        def act():
            mine = lax.rem(me_s, owners)
            whole(inbox, NS - 1, sems[0], sems[1]).wait_recv()
            acc = part[mine]
            for d in range(1, NS):
                acc = acc + inbox[lax.rem(me_s + d, NS)]
            total[mine] = acc
            for d in range(1, NS):
                pltpu.make_async_remote_copy(
                    src_ref=total.at[mine], dst_ref=total.at[mine],
                    send_sem=sems[2], recv_sem=sems[3],
                    device_id={"space": lax.rem(me_s + d, NS)}, device_id_type=MESH,
                ).start()

        if owners == NS:
            act()
        else:
            pl.when(me_s < owners)(act)

    def take(total, sems, owners):
        others(owners, lambda count: whole(total, count, sems[2], sems[3]).wait_recv())

    def settle(inbox, sems, owners):
        others(owners, lambda count: whole(inbox, count, sems[0], sems[1]).wait_send())
        finish = whole(inbox, NS - 1, sems[2], sems[3]).wait_send
        if owners == NS:
            finish()
        else:
            pl.when(me_s < owners)(finish)

    spread(part2, inbox2, sems2, OWNERS2)

    def unpack(wide, at):
        for j in range(SEGS):
            rows[at : at + M, j * LANES : (j + 1) * LANES] = wide[pl.ds(j, M, stride=SEGS), :].astype(jnp.bfloat16)

    whole(got1, GROUP - 1, send1_sem, recv1_sem).wait_recv()
    for peer in peers1:
        widen(wide1, got1, peer - first)
    unpack(wide1, X1)
    whole(got0, NZ, sendy_sem, recvy_sem).wait_recv()
    for zz in (*turn, z):
        widen(wide0, got0, 2 * zz + 1 - h)
    unpack(wide0, X0)

    both = dot_nt(rows[:X2], rows[X0:X2])
    mine = turned[LANE1:, : 2 * M]
    by_field = exact(mine, both[:STEPS], ((1,), (1,)))
    by_modes = exact(exact(mine, both[STEPS:], ((1,), (1,))), chosen[: 2 * M])
    put(
        part01,
        [by_field[:, :LANES], jnp.concatenate([by_field[:, LANES:], by_modes[:, LANE1:]], axis=1)],
    )
    spread(part01, inbox01, sems01, NS)
    reduce(part2, inbox2, total2, sems2, OWNERS2)
    reduce(part01, inbox01, total01, sems01, NS)
    take(total2, sems2, OWNERS2)
    sums[16:] = total2[...]
    take(total01, sems01, NS)
    sums[:16] = total01[...]

    whole(got0, NZ - 1, send0_sem, recv0_sem.at[z]).wait_send()
    whole(got0, NZ, sendy_sem, recvy_sem).wait_send()
    whole(got1, GROUP - 1, send1_sem, recv1_sem).wait_send()
    settle(inbox2, sems2, OWNERS2)
    settle(inbox01, sems01, NS)


def eliminate(tiles, pivot_tile, pivot_lane):
    sub = lax.broadcasted_iota(jnp.int32, (8, LANES), 0)
    over = lambda x, i: jnp.broadcast_to(x[i : i + 1], (8, LANES))
    count = len(tiles[0])
    ahead = {}
    for k in range(0, R, 2):
        g, i = divmod(k, 8)
        for j in range(k, min(k + 2 * AHEAD + 2, R)):
            if j not in ahead:
                lane = pivot_lane + j
                ahead[j] = [jnp.broadcast_to(row[pivot_tile][:, lane : lane + 1], (8, LANES)) for row in tiles]
        left, right = ahead.pop(k), ahead.pop(k + 1)
        a, b, c, d = over(left[g], i), over(right[g], i), over(left[g], i + 1), over(right[g], i + 1)
        scale = 1.0 / (a * d - b * c)
        a, b, c, d = a * scale, b * scale, c * scale, d * scale

        def pivot(old):
            first, second = over(old[g], i), over(old[g], i + 1)
            upper, lower = d * first - b * second, a * second - c * first
            moved = [old[q] - (left[q] * upper + right[q] * lower) for q in range(len(old))]
            moved[g] = jnp.where(sub == i, upper, jnp.where(sub == i + 1, lower, moved[g]))
            return moved

        ahead = {j: pivot(old) for j, old in ahead.items()}
        columns = [pivot([row[t] for row in tiles]) for t in range(count)]
        tiles = [[columns[t][q] for t in range(count)] for q in range(R // 8)]
    return tiles


def solve(block, pivot):
    tile, at = divmod(pivot, LANES)
    sub = lax.broadcasted_iota(jnp.int32, (8, LANES), 0)
    lane = lax.broadcasted_iota(jnp.int32, (8, LANES), 1)
    tiles = [
        [block[8 * g : 8 * (g + 1), LANES * t : LANES * (t + 1)] for t in range(block.shape[1] // LANES)]
        for g in range(R // 8)
    ]
    for g in range(R // 8):
        tiles[g][tile] = jnp.where(lane == at + 8 * g + sub, tiles[g][tile] + EPS, tiles[g][tile])
    done = eliminate(tiles, tile, at)
    return jnp.concatenate([jnp.concatenate(row, axis=1) for row in done], axis=0)


def update(sums, chosen, among, rows, record, out_hbm, field, out, weights, load_sem, store_sem):
    load = pltpu.make_async_copy(record, field, load_sem)
    load.start()
    scale = 1.0 / (POINTS * NS)
    tall = lambda first, t: jnp.concatenate([sums[first + 2 * g + t] for g in range(R // 8)], axis=0) * scale
    blocks = []
    for first in (8, 0, 16):
        left, right = tall(first, 0), tall(first, 1)
        by_field = jnp.concatenate([left, right], axis=1)[:, :STEPS]
        blocks.append(jnp.concatenate([left, right, exact(by_field, among[...])], axis=1))
    at1, at0, at2 = LANES + LANE1, LANES + LANE0, 2 * LANES

    def change(level, done, at):
        cols = slice(at, at + R)
        return exact(blocks[level][:, cols] + EPS * done[:, cols], done, ((0,), (0,)))

    done0 = solve(blocks[0], at0)
    blocks[1] = blocks[1] - change(0, done0, at1)
    blocks[2] = blocks[2] - change(0, done0, at2)
    done1 = solve(blocks[1], at1)
    blocks[2] = blocks[2] - change(1, done1, at2)
    pick0 = chosen[:M, LANE0 : LANE0 + R]
    pick1 = chosen[M : 2 * M, LANE1 : LANE1 + R]
    pick2 = chosen[2 * M :, :R]
    way0 = pick0
    way1 = -exact(pick0, done0[:, at1 : at1 + R])
    way2 = -exact(pick0, done0[:, at2 : at2 + R]) - exact(way1, done1[:, at2 : at2 + R])
    low2 = -exact(pick1, done1[:, at2 : at2 + R])
    part0 = exact(done0[:, :STEPS], way0, ((0,), (1,))) + exact(done1[:, :STEPS], way1, ((0,), (1,)))
    part1 = exact(done1[:, :STEPS], pick1, ((0,), (1,)))
    last = jnp.concatenate([way2, low2, pick2], axis=0)
    early = jnp.concatenate([part0, part1, jnp.zeros((STEPS, 2 * M), jnp.float32)], axis=1)
    done2 = solve(blocks[2], at2)
    slopes = early + exact(done2[:, :STEPS], last, ((0,), (1,)))
    high = slopes.astype(jnp.bfloat16)
    weights[:STEPS] = high
    weights[STEPS:] = (slopes - high.astype(jnp.float32)).astype(jnp.bfloat16)
    load.wait()
    stores = []
    for c in range(POINTS // WIDTH):
        cols = slice(c * WIDTH, (c + 1) * WIDTH)
        slow = jnp.dot(weights[...], rows[X0:, cols], preferred_element_type=jnp.float32)
        out[:, cols] = field[:, cols] - (slow[:STEPS] + slow[STEPS:])
        store = pltpu.make_async_copy(out.at[:, cols], out_hbm.at[:, cols], store_sem.at[c])
        store.start()
        stores.append(store)
    for store in stores:
        store.wait()


def body(record, mode_basis, slow_picks, phases):
    dma = pltpu.SemaphoreType.DMA
    vmem = pl.BlockSpec(memory_space=pltpu.VMEM)
    hbm = pl.BlockSpec(memory_space=pltpu.MemorySpace.HBM)
    tiled = record.reshape(TILES, 8, SEGS, LANES).transpose(0, 2, 1, 3).reshape(TILES // 2, 2, BLOCK, LANES)
    far = lambda x: pltpu.with_memory_space_constraint(x, pltpu.MemorySpace.HBM)
    chunk = lambda count: pltpu.VMEM((count, 8, LANES), jnp.float32)
    rows, sums, chosen, among = pl.pallas_call(
        collect,
        out_shape=[
            pltpu.VMEM((ALL, POINTS), jnp.bfloat16),
            pltpu.VMEM((24, 8, LANES), jnp.float32),
            pltpu.VMEM((4 * M, LANES), jnp.float32),
            pltpu.VMEM((STEPS, LANES), jnp.float32),
        ],
        in_specs=[hbm] * 4,
        out_specs=[vmem] * 4,
        scratch_shapes=[
            pltpu.SMEM((21,), jnp.int32),
            pltpu.VMEM((21, R), jnp.int32),
            pltpu.VMEM((TILES // 2 * BLOCK, LANES), jnp.float32),
            pltpu.VMEM((TILES // 2 * BLOCK, LANES), jnp.float32),
            pltpu.VMEM((NT, ROWS0 * SEGS, LANES), jnp.bfloat16),
            pltpu.VMEM((GROUP, ROWS1 * SEGS, LANES), jnp.bfloat16),
            pltpu.VMEM((M * SEGS, LANES), jnp.float32),
            pltpu.VMEM((M * SEGS, LANES), jnp.float32),
            pltpu.VMEM((3, M, M), jnp.float32),
            pltpu.VMEM((LANES, 4 * M), jnp.float32),
            pltpu.VMEM((M, LANES), jnp.float32),
            chunk(8), chunk(NS), chunk(8), chunk(16), chunk(NS), chunk(16),
            dma((2,)), dma((5,)), dma((NZ,)), dma((13,)),
        ],
        compiler_params=pltpu.CompilerParams(
            collective_id=0, has_side_effects=True, vmem_limit_bytes=VMEM_LIMIT
        ),
        name="collect",
    )(far(phases), far(slow_picks), far(mode_basis), far(tiled))
    near = lambda x: pltpu.with_memory_space_constraint(x, pltpu.VMEM)
    return pl.pallas_call(
        update,
        out_shape=jax.ShapeDtypeStruct((STEPS, POINTS), jnp.float32),
        in_specs=[vmem, vmem, vmem, vmem, hbm],
        out_specs=hbm,
        scratch_shapes=[
            pltpu.VMEM((STEPS, POINTS), jnp.float32),
            pltpu.VMEM((STEPS, POINTS), jnp.float32),
            pltpu.VMEM((2 * STEPS, 4 * M), jnp.bfloat16),
            dma(()), dma((POINTS // WIDTH,)),
        ],
        compiler_params=pltpu.CompilerParams(vmem_limit_bytes=VMEM_LIMIT),
        name="update",
    )(near(sums), near(chosen), near(among), near(rows), far(record))


def solution(mesh):
    in_specs = (P("tm", "space"), P(), P(), P())
    return jax.shard_map(body, mesh=mesh, in_specs=in_specs, out_specs=P("tm", "space"), check_vma=False)
```

```python
import jax
import jax.numpy as jnp
from jax import lax
from jax.experimental import pallas as pl
from jax.experimental.pallas import tpu as pltpu
from jax.sharding import PartitionSpec as P

M = 48
R = 32
LANES = 128
WIDTH = 512
EPS = 1e-5
AHEAD = 4
MESH = pl.DeviceIdType.MESH
EXACT = lax.Precision.HIGHEST
VMEM_LIMIT = 24 * 1024 * 1024
NT = 16
NS = 16
NZ = NT // 2
CHIPS = NS // 2
GROUP = 4
STEPS = 192
POINTS = 4096
SEGS = POINTS // LANES
TILES = STEPS // 8
BLOCK = SEGS * 8
ROWS0 = M // NT
ROWS1 = M // GROUP
X0 = STEPS
X1 = X0 + M
X2 = X1 + M
ALL = X2 + 2 * M
LANE1 = 64
LANE0 = 96
OWNERS2 = 8


def dot_nt(a, b):
    return lax.dot_general(a, b, (((1,), (1,)), ((), ())), preferred_element_type=jnp.float32)


def exact(a, b, dims=((1,), (0,))):
    return lax.dot_general(a, b, (dims, ((), ())), precision=EXACT, preferred_element_type=jnp.float32)


def collect(
    phases_hbm, picks_hbm, basis_hbm, record,
    rows, sums, chosen, among,
    phases, picks, head, field_even, field_odd, got0, got1, wide0, wide1, basis, turned, pad,
    part2, inbox2, total2, part01, inbox_mate, halves, total01,
    load_sem, small_sem, recv0_sem, sem,
):
    send0_sem, sendy_sem, recvy_sem, send1_sem, recv1_sem = [sem.at[i] for i in range(5)]
    recvp_sem = sem.at[15]
    sems2 = [sem.at[i] for i in range(5, 9)]
    mate_sems, chip_sems, back_sems = [[sem.at[j], sem.at[j + 1]] for j in (9, 11, 13)]
    me_t = lax.axis_index("tm")
    me_s = lax.axis_index("space")
    first = me_t // GROUP * GROUP

    barrier = pltpu.get_barrier_semaphore()
    for d in range(1, NT):
        pl.semaphore_signal(barrier, inc=1, device_id={"tm": lax.rem(me_t + d, NT)}, device_id_type=MESH)
    for d in range(1, NS):
        pl.semaphore_signal(barrier, inc=1, device_id={"space": lax.rem(me_s + d, NS)}, device_id_type=MESH)

    get_phases = pltpu.make_async_copy(phases_hbm, phases, small_sem.at[3])
    get_phases.start()
    load_even, load_odd = [
        pltpu.make_async_copy(record.at[:, :, i], half.reshape(ROWS0, ROWS1 // ROWS0, BLOCK, LANES), load_sem.at[i])
        for i, half in enumerate((field_even, field_odd))
    ]
    load_head = pltpu.make_async_copy(record.at[:, 0, 0], head.reshape(ROWS0, BLOCK, LANES), load_sem.at[2])
    load_head.start()
    load_even.start()
    q1 = 1 + me_t // GROUP
    q2 = 5 + me_t
    fetches = [
        pltpu.make_async_copy(basis_hbm.at[q], basis.at[level], small_sem.at[level])
        for level, q in enumerate((0, q1, q2))
    ]
    fetches.append(pltpu.make_async_copy(picks_hbm, picks, small_sem.at[4]))
    for fetch in fetches:
        fetch.start()
    load_odd.start()

    get_phases.wait()
    off0 = lax.rem(phases[0], STEPS * NT // M)
    off1 = lax.rem(phases[q1], STEPS * GROUP // M)
    off2 = lax.rem(phases[q2], STEPS // M)
    load_head.wait()
    for r in range(ROWS0):
        got0[me_t, r * SEGS : (r + 1) * SEGS] = head[pl.ds(r * BLOCK + off0, SEGS, stride=8), :].astype(jnp.bfloat16)

    pl.semaphore_wait(barrier, NT - 1 + NS - 1)

    z = me_t // 2
    h = lax.rem(me_t, 2)
    partner = me_t + 1 - 2 * h
    near = me_t + 2 - 4 * lax.rem(z, 2)
    across = near + 1 - 2 * h

    def along0(target, owner, send_sem, recv_sem):
        return pltpu.make_async_remote_copy(
            src_ref=got0.at[owner], dst_ref=got0.at[owner], send_sem=send_sem, recv_sem=recv_sem,
            device_id={"tm": target}, device_id_type=MESH,
        )

    def along1(target, owner, recv_sem):
        return pltpu.make_async_remote_copy(
            src_ref=got1.at[owner - first], dst_ref=got1.at[owner - first],
            send_sem=send1_sem, recv_sem=recv_sem,
            device_id={"tm": target}, device_id_type=MESH,
        )

    def whole(ref, count, send_sem, recv_sem):
        place = ref.at[pl.ds(0, count)]
        return pltpu.make_async_remote_copy(
            src_ref=place, dst_ref=place, send_sem=send_sem, recv_sem=recv_sem,
            device_id={"tm": partner}, device_id_type=MESH,
        )

    hops = (1, -1, 2, -2, 3, -3, 4)
    turn = [lax.rem(z + d + NZ, NZ) for d in hops]
    out0 = [along0(2 * turn[i] + h, me_t, send0_sem, recv0_sem.at[z]) for i in range(7)]
    in0 = [along0(2 * turn[i] + h, 2 * turn[i] + h, send0_sem, recv0_sem.at[turn[i]]) for i in range(7)]
    over0 = [along0(partner, 2 * turn[i] + h, sendy_sem, recvy_sem) for i in range(7)]
    over0.append(along0(partner, me_t, sendy_sem, recvy_sem))
    peers1 = (near, partner, across)
    out1 = [along1(near, me_t, recv1_sem), along1(partner, me_t, recvp_sem), along1(near, partner, recv1_sem)]
    in_partner = along1(partner, partner, recvp_sem)
    for copy in (over0[7], *out0):
        copy.start()
    load_even.wait()
    for r in range(ROWS1):
        got1[me_t - first, r * SEGS : (r + 1) * SEGS] = field_even[
            pl.ds(r * BLOCK + off1, SEGS, stride=8), :
        ].astype(jnp.bfloat16)
    for copy in (out1[1], out1[0]):
        copy.start()

    def widen(wide, got, slot):
        count = got.shape[1] // SEGS
        for r in range(count):
            wide[pl.ds(slot * count + r, SEGS, stride=M), :] = got[slot, r * SEGS : (r + 1) * SEGS].astype(jnp.float32)

    def pass0(i):
        in0[i].wait_recv()
        over0[i].start()
        widen(wide0, got0, 2 * turn[i] + h)

    load_odd.wait()

    def part_columns(c, carry):
        cols = pl.ds(pl.multiple_of(c * LANES, LANES), LANES)
        at = pl.multiple_of(c * 8, 8)
        for p in range(TILES // 2):
            pair = jnp.concatenate(
                [field_even[pl.ds(p * BLOCK + at, 8), :], field_odd[pl.ds(p * BLOCK + at, 8), :]], axis=0
            )
            rows[16 * p : 16 * (p + 1), cols] = pair.astype(jnp.bfloat16)
        x2 = jnp.concatenate(
            [
                half[pl.ds(at + off2 + more, TILES // 2, stride=BLOCK), :]
                for half in (field_even, field_odd)
                for more in (0, 4)
            ],
            axis=0,
        )
        high2 = x2.astype(jnp.bfloat16)
        rows[X2 : X2 + M, cols] = high2
        rows[X2 + M :, cols] = (x2 - high2.astype(jnp.float32)).astype(jnp.bfloat16)
        return carry

    lax.fori_loop(0, SEGS, part_columns, 0)
    widen(wide0, got0, me_t)
    widen(wide1, got1, me_t - first)

    for fetch in fetches:
        fetch.wait()
    none = lambda count: [jnp.full((1, R), -1, jnp.int32)] * count
    row_m = lax.broadcasted_iota(jnp.int32, (M, LANES), 0)
    for level, (q, place, at) in enumerate(((0, 3, 0), (q1, 2, M), (q2, 0, 2 * M))):
        spots = jnp.concatenate([*none(place), picks[pl.ds(q, 1), :], *none(3 - place)], axis=1)
        columns = exact(basis[level], (row_m == spots).astype(jnp.float32))
        if level == 2:
            pad[...] = columns
            columns = jnp.concatenate([pad[pl.ds(i, M // 4, stride=4), :] for i in range(4)], axis=0)
            chosen[3 * M :] = columns
        chosen[at : at + M] = columns
    turned[...] = chosen[...].T
    at_row = lax.broadcasted_iota(jnp.int32, (STEPS, M), 0)
    order = lax.broadcasted_iota(jnp.int32, (STEPS, M), 1)
    rank = lax.rem(order, M // 4) * 4 + order // (M // 4)
    among[...] = exact((at_row == 4 * rank + off2).astype(jnp.float32), chosen[2 * M : 3 * M])
    def put(ref, tiles):
        for g in range(tiles[0].shape[0] // 8):
            for t in range(2):
                ref[2 * g + t] = tiles[t][8 * g : 8 * (g + 1)]

    space = jnp.zeros((R, 2 * LANES - STEPS), jnp.float32)
    by_field2 = exact(turned[:R, 2 * M :], dot_nt(rows[:STEPS], rows[X2:]), ((1,), (1,)))
    put(part2, [by_field2[:, :LANES], jnp.concatenate([by_field2[:, LANES:], space], axis=1)])

    def others(do):
        pl.when(me_s < OWNERS2)(lambda: do(OWNERS2 - 1))
        pl.when(me_s >= OWNERS2)(lambda: do(OWNERS2))

    for d in range(1, NS):
        tgt = lax.rem(me_s + d, NS)
        copy = pltpu.make_async_remote_copy(
            src_ref=part2.at[lax.rem(tgt, OWNERS2)], dst_ref=inbox2.at[me_s],
            send_sem=sems2[0], recv_sem=sems2[1],
            device_id={"space": tgt}, device_id_type=MESH,
        )
        pl.when(tgt < OWNERS2)(copy.start)

    for i in range(7):
        pass0(i)
        if i == 3:
            in_partner.wait_recv()
            out1[2].start()

    @pl.when(me_s < OWNERS2)
    def _():
        own = lax.rem(me_s, OWNERS2)
        whole(inbox2, NS - 1, sems2[0], sems2[1]).wait_recv()
        acc = part2[own]
        for d in range(1, NS):
            acc = acc + inbox2[lax.rem(me_s + d, NS)]
        total2[own] = acc
        for d in range(1, NS):
            pltpu.make_async_remote_copy(
                src_ref=total2.at[own], dst_ref=total2.at[own], send_sem=sems2[2], recv_sem=sems2[3],
                device_id={"space": lax.rem(me_s + d, NS)}, device_id_type=MESH,
            ).start()

    def unpack(wide, at):
        for j in range(SEGS):
            rows[at : at + M, j * LANES : (j + 1) * LANES] = wide[j * M : (j + 1) * M].astype(jnp.bfloat16)

    whole(got1, 2, send1_sem, recv1_sem).wait_recv()
    for peer in peers1:
        widen(wide1, got1, peer - first)
    unpack(wide1, X1)
    whole(got0, NZ, sendy_sem, recvy_sem).wait_recv()
    for zz in (*turn, z):
        widen(wide0, got0, 2 * zz + 1 - h)
    unpack(wide0, X0)

    both = dot_nt(rows[:X2], rows[X0:X2])
    mine = turned[LANE1:, : 2 * M]
    by_field = exact(mine, both[:STEPS], ((1,), (1,)))
    by_modes = exact(exact(mine, both[STEPS:], ((1,), (1,))), chosen[: 2 * M])
    put(
        part01,
        [by_field[:, :LANES], jnp.concatenate([by_field[:, LANES:], by_modes[:, LANE1:]], axis=1)],
    )

    core = lax.rem(me_s, 2)
    chip = me_s // 2
    mate = me_s + 1 - 2 * core
    mine = pl.ds(core * 8, 8)

    def to_mate(src, dst, sems):
        return pltpu.make_async_remote_copy(
            src_ref=src, dst_ref=dst, send_sem=sems[0], recv_sem=sems[1],
            device_id={"space": mate}, device_id_type=MESH,
        )

    give = to_mate(part01.at[pl.ds(8 - core * 8, 8)], inbox_mate, mate_sems)
    give.start()
    give.wait_recv()
    halves[chip] = part01[mine] + inbox_mate[...]
    for d in range(1, CHIPS):
        pltpu.make_async_remote_copy(
            src_ref=halves.at[chip], dst_ref=halves.at[chip], send_sem=chip_sems[0], recv_sem=chip_sems[1],
            device_id={"space": 2 * lax.rem(chip + d, CHIPS) + core}, device_id_type=MESH,
        ).start()
    whole(halves, CHIPS - 1, chip_sems[0], chip_sems[1]).wait_recv()
    acc = halves[0]
    for i in range(1, CHIPS):
        acc = acc + halves[i]
    total01[mine] = acc
    back = to_mate(total01.at[mine], total01.at[mine], back_sems)
    back.start()
    others(lambda count: whole(total2, count, sems2[2], sems2[3]).wait_recv())
    sums[16:] = total2[...]
    back.wait_recv()
    sums[:16] = total01[...]

    whole(got0, NZ - 1, send0_sem, recv0_sem.at[z]).wait_send()
    whole(got0, NZ, sendy_sem, recvy_sem).wait_send()
    whole(got1, GROUP - 1, send1_sem, recv1_sem).wait_send()
    others(lambda count: whole(inbox2, count, sems2[0], sems2[1]).wait_send())
    pl.when(me_s < OWNERS2)(whole(inbox2, NS - 1, sems2[2], sems2[3]).wait_send)
    give.wait_send()
    whole(halves, CHIPS - 1, chip_sems[0], chip_sems[1]).wait_send()
    back.wait_send()


def eliminate(tiles, pivot_tile, pivot_lane):
    sub = lax.broadcasted_iota(jnp.int32, (8, LANES), 0)
    over = lambda x, i: jnp.broadcast_to(x[i : i + 1], (8, LANES))
    count = len(tiles[0])
    ahead = {}
    for k in range(0, R, 2):
        g, i = divmod(k, 8)
        for j in range(k, min(k + 2 * AHEAD + 2, R)):
            if j not in ahead:
                lane = pivot_lane + j
                ahead[j] = [jnp.broadcast_to(row[pivot_tile][:, lane : lane + 1], (8, LANES)) for row in tiles]
        left, right = ahead.pop(k), ahead.pop(k + 1)
        a, b, c, d = over(left[g], i), over(right[g], i), over(left[g], i + 1), over(right[g], i + 1)
        scale = 1.0 / (a * d - b * c)
        a, b, c, d = a * scale, b * scale, c * scale, d * scale

        def pivot(old):
            first, second = over(old[g], i), over(old[g], i + 1)
            upper, lower = d * first - b * second, a * second - c * first
            moved = [old[q] - (left[q] * upper + right[q] * lower) for q in range(len(old))]
            moved[g] = jnp.where(sub == i, upper, jnp.where(sub == i + 1, lower, moved[g]))
            return moved

        ahead = {j: pivot(old) for j, old in ahead.items()}
        columns = [pivot([row[t] for row in tiles]) for t in range(count)]
        tiles = [[columns[t][q] for t in range(count)] for q in range(R // 8)]
    return tiles


def solve(block, pivot):
    tile, at = divmod(pivot, LANES)
    sub = lax.broadcasted_iota(jnp.int32, (8, LANES), 0)
    lane = lax.broadcasted_iota(jnp.int32, (8, LANES), 1)
    tiles = [
        [block[8 * g : 8 * (g + 1), LANES * t : LANES * (t + 1)] for t in range(block.shape[1] // LANES)]
        for g in range(R // 8)
    ]
    for g in range(R // 8):
        tiles[g][tile] = jnp.where(lane == at + 8 * g + sub, tiles[g][tile] + EPS, tiles[g][tile])
    done = eliminate(tiles, tile, at)
    return jnp.concatenate([jnp.concatenate(row, axis=1) for row in done], axis=0)


def update(sums, chosen, among, rows, record, out_hbm, field, out, weights, held, load_sem, store_sem):
    live = lax.axis_index("tm") >= 0

    load = pltpu.make_async_copy(record, field, load_sem)
    load.start()
    @pl.when(live)
    def _():
        scale = 1.0 / (POINTS * NS)
        tall = lambda first, t: jnp.concatenate([sums[first + 2 * g + t] for g in range(R // 8)], axis=0) * scale
        blocks = []
        for first in (8, 0, 16):
            left, right = tall(first, 0), tall(first, 1)
            by_field = jnp.concatenate([left, right], axis=1)[:, :STEPS]
            blocks.append(jnp.concatenate([left, right, exact(by_field, among[...])], axis=1))
        for level in range(3):
            held[level] = blocks[level]

    @pl.when(live)
    def _():
        blocks = [held[level] for level in range(3)]
        at1, at0, at2 = LANES + LANE1, LANES + LANE0, 2 * LANES

        def change(level, done, at):
            cols = slice(at, at + R)
            return exact(blocks[level][:, cols] + EPS * done[:, cols], done, ((0,), (0,)))

        done0 = solve(blocks[0], at0)
        blocks[1] = blocks[1] - change(0, done0, at1)
        blocks[2] = blocks[2] - change(0, done0, at2)
        done1 = solve(blocks[1], at1)
        blocks[2] = blocks[2] - change(1, done1, at2)
        pick0 = chosen[:M, LANE0 : LANE0 + R]
        pick1 = chosen[M : 2 * M, LANE1 : LANE1 + R]
        pick2 = chosen[2 * M :, :R]
        way0 = pick0
        way1 = -exact(pick0, done0[:, at1 : at1 + R])
        way2 = -exact(pick0, done0[:, at2 : at2 + R]) - exact(way1, done1[:, at2 : at2 + R])
        low2 = -exact(pick1, done1[:, at2 : at2 + R])
        part0 = exact(done0[:, :STEPS], way0, ((0,), (1,))) + exact(done1[:, :STEPS], way1, ((0,), (1,)))
        part1 = exact(done1[:, :STEPS], pick1, ((0,), (1,)))
        last = jnp.concatenate([way2, low2, pick2], axis=0)
        early = jnp.concatenate([part0, part1, jnp.zeros((STEPS, 2 * M), jnp.float32)], axis=1)
        done2 = solve(blocks[2], at2)
        slopes = early + exact(done2[:, :STEPS], last, ((0,), (1,)))
        high = slopes.astype(jnp.bfloat16)
        weights[:STEPS] = high
        weights[STEPS:] = (slopes - high.astype(jnp.float32)).astype(jnp.bfloat16)

    load.wait()
    stores = []
    for c in range(POINTS // WIDTH):
        cols = slice(c * WIDTH, (c + 1) * WIDTH)
        slow = jnp.dot(weights[...], rows[X0:, cols], preferred_element_type=jnp.float32)
        out[:, cols] = field[:, cols] - (slow[:STEPS] + slow[STEPS:])
        store = pltpu.make_async_copy(out.at[:, cols], out_hbm.at[:, cols], store_sem.at[c])
        store.start()
        stores.append(store)
    for store in stores:
        store.wait()


def body(record, mode_basis, slow_picks, phases):
    dma = pltpu.SemaphoreType.DMA
    vmem = pl.BlockSpec(memory_space=pltpu.VMEM)
    hbm = pl.BlockSpec(memory_space=pltpu.MemorySpace.HBM)
    tiled = record.reshape(TILES, 8, SEGS, LANES).transpose(0, 2, 1, 3).reshape(ROWS0, ROWS1 // ROWS0, 2, BLOCK, LANES)
    far = lambda x: pltpu.with_memory_space_constraint(x, pltpu.MemorySpace.HBM)
    chunk = lambda *count: pltpu.VMEM((*count, 8, LANES), jnp.float32)
    rows, sums, chosen, among = pl.pallas_call(
        collect,
        out_shape=[
            pltpu.VMEM((ALL, POINTS), jnp.bfloat16),
            pltpu.VMEM((24, 8, LANES), jnp.float32),
            pltpu.VMEM((4 * M, LANES), jnp.float32),
            pltpu.VMEM((STEPS, LANES), jnp.float32),
        ],
        in_specs=[hbm] * 4,
        out_specs=[vmem] * 4,
        scratch_shapes=[
            pltpu.SMEM((21,), jnp.int32),
            pltpu.VMEM((21, R), jnp.int32),
            pltpu.VMEM((ROWS0 * BLOCK, LANES), jnp.float32),
            pltpu.VMEM((TILES // 2 * BLOCK, LANES), jnp.float32),
            pltpu.VMEM((TILES // 2 * BLOCK, LANES), jnp.float32),
            pltpu.VMEM((NT, ROWS0 * SEGS, LANES), jnp.bfloat16),
            pltpu.VMEM((GROUP, ROWS1 * SEGS, LANES), jnp.bfloat16),
            pltpu.VMEM((M * SEGS, LANES), jnp.float32),
            pltpu.VMEM((M * SEGS, LANES), jnp.float32),
            pltpu.VMEM((3, M, M), jnp.float32),
            pltpu.VMEM((LANES, 4 * M), jnp.float32),
            pltpu.VMEM((M, LANES), jnp.float32),
            chunk(8), chunk(NS), chunk(8), chunk(16), chunk(8), chunk(CHIPS, 8), chunk(16),
            dma((3,)), dma((5,)), dma((NZ,)), dma((16,)),
        ],
        compiler_params=pltpu.CompilerParams(
            collective_id=0, has_side_effects=True, vmem_limit_bytes=VMEM_LIMIT
        ),
        name="collect",
    )(far(phases), far(slow_picks), far(mode_basis), far(tiled))
    near = lambda x: pltpu.with_memory_space_constraint(x, pltpu.VMEM)
    return pl.pallas_call(
        update,
        out_shape=jax.ShapeDtypeStruct((STEPS, POINTS), jnp.float32),
        in_specs=[vmem, vmem, vmem, vmem, hbm],
        out_specs=hbm,
        scratch_shapes=[
            pltpu.VMEM((STEPS, POINTS), jnp.float32),
            pltpu.VMEM((STEPS, POINTS), jnp.float32),
            pltpu.VMEM((2 * STEPS, 4 * M), jnp.bfloat16),
            pltpu.VMEM((3, R, 3 * LANES), jnp.float32),
            dma(()), dma((POINTS // WIDTH,)),
        ],
        compiler_params=pltpu.CompilerParams(vmem_limit_bytes=VMEM_LIMIT),
        name="update",
    )(near(sums), near(chosen), near(among), near(rows), far(record))


def solution(mesh):
    in_specs = (P("tm", "space"), P(), P(), P())
    return jax.shard_map(body, mesh=mesh, in_specs=in_specs, out_specs=P("tm", "space"), check_vma=False)
```

```python
import jax
import jax.numpy as jnp
from jax import lax
from jax.experimental import pallas as pl
from jax.experimental.pallas import tpu as pltpu
from jax.sharding import PartitionSpec as P

M = 48
R = 32
LANES = 128
WIDTH = 512
EPS = 1e-5
AHEAD = 4
MESH = pl.DeviceIdType.MESH
EXACT = lax.Precision.HIGHEST
VMEM_LIMIT = 24 * 1024 * 1024
NT = 16
NS = 16
NZ = NT // 2
CHIPS = NS // 2
GROUP = 4
STEPS = 192
POINTS = 4096
SEGS = POINTS // LANES
TILES = STEPS // 8
BLOCK = SEGS * 8
ROWS0 = M // NT
ROWS1 = M // GROUP
X0 = STEPS
X1 = X0 + M
X2 = X1 + M
ALL = X2 + 2 * M
LANE1 = 64
LANE0 = 96
OWNERS2 = 8


def dot_nt(a, b):
    return lax.dot_general(a, b, (((1,), (1,)), ((), ())), preferred_element_type=jnp.float32)


def exact(a, b, dims=((1,), (0,))):
    return lax.dot_general(a, b, (dims, ((), ())), precision=EXACT, preferred_element_type=jnp.float32)


def collect(
    phases_hbm, picks_hbm, basis_hbm, record,
    rows, sums, chosen, among,
    phases, picks, head, field_even, field_odd, got0, got1, wide0, wide1, basis, turned, pad,
    part2, inbox2, total2, part01, inbox_mate, halves, total01,
    load_sem, small_sem, recv0_sem, sem,
):
    send0_sem, sendy_sem, recvy_sem, send1_sem, recv1_sem = [sem.at[i] for i in range(5)]
    recvp_sem = sem.at[15]
    sems2 = [sem.at[i] for i in range(5, 9)]
    mate_sems, chip_sems, back_sems = [[sem.at[j], sem.at[j + 1]] for j in (9, 11, 13)]
    me_t = lax.axis_index("tm")
    me_s = lax.axis_index("space")
    first = me_t // GROUP * GROUP

    barrier = pltpu.get_barrier_semaphore()
    for d in range(1, NT):
        pl.semaphore_signal(barrier, inc=1, device_id={"tm": lax.rem(me_t + d, NT)}, device_id_type=MESH)
    for d in range(1, NS):
        pl.semaphore_signal(barrier, inc=1, device_id={"space": lax.rem(me_s + d, NS)}, device_id_type=MESH)

    get_phases = pltpu.make_async_copy(phases_hbm, phases, small_sem.at[3])
    get_phases.start()
    load_even, load_odd = [
        pltpu.make_async_copy(record.at[:, :, i], half.reshape(ROWS0, ROWS1 // ROWS0, BLOCK, LANES), load_sem.at[i])
        for i, half in enumerate((field_even, field_odd))
    ]
    load_head = pltpu.make_async_copy(record.at[:, 0, 0], head.reshape(ROWS0, BLOCK, LANES), load_sem.at[2])
    load_head.start()
    load_even.start()
    q1 = 1 + me_t // GROUP
    q2 = 5 + me_t
    fetches = [
        pltpu.make_async_copy(basis_hbm.at[q], basis.at[level], small_sem.at[level])
        for level, q in enumerate((0, q1, q2))
    ]
    fetches.append(pltpu.make_async_copy(picks_hbm, picks, small_sem.at[4]))
    for fetch in fetches:
        fetch.start()
    load_odd.start()

    get_phases.wait()
    off0 = lax.rem(phases[0], STEPS * NT // M)
    off1 = lax.rem(phases[q1], STEPS * GROUP // M)
    off2 = lax.rem(phases[q2], STEPS // M)
    load_head.wait()
    for r in range(ROWS0):
        got0[me_t, r * SEGS : (r + 1) * SEGS] = head[pl.ds(r * BLOCK + off0, SEGS, stride=8), :].astype(jnp.bfloat16)

    pl.semaphore_wait(barrier, NT - 1 + NS - 1)

    z = me_t // 2
    h = lax.rem(me_t, 2)
    partner = me_t + 1 - 2 * h
    near = me_t + 2 - 4 * lax.rem(z, 2)
    across = near + 1 - 2 * h

    def along0(target, owner, send_sem, recv_sem):
        return pltpu.make_async_remote_copy(
            src_ref=got0.at[owner], dst_ref=got0.at[owner], send_sem=send_sem, recv_sem=recv_sem,
            device_id={"tm": target}, device_id_type=MESH,
        )

    def along1(target, owner, recv_sem):
        return pltpu.make_async_remote_copy(
            src_ref=got1.at[owner - first], dst_ref=got1.at[owner - first],
            send_sem=send1_sem, recv_sem=recv_sem,
            device_id={"tm": target}, device_id_type=MESH,
        )

    def whole(ref, count, send_sem, recv_sem):
        place = ref.at[pl.ds(0, count)]
        return pltpu.make_async_remote_copy(
            src_ref=place, dst_ref=place, send_sem=send_sem, recv_sem=recv_sem,
            device_id={"tm": partner}, device_id_type=MESH,
        )

    hops = (1, -1, 2, -2, 3, -3, 4)
    turn = [lax.rem(z + d + NZ, NZ) for d in hops]
    out0 = [along0(2 * turn[i] + h, me_t, send0_sem, recv0_sem.at[z]) for i in range(7)]
    in0 = [along0(2 * turn[i] + h, 2 * turn[i] + h, send0_sem, recv0_sem.at[turn[i]]) for i in range(7)]
    over0 = [along0(partner, 2 * turn[i] + h, sendy_sem, recvy_sem) for i in range(7)]
    over0.append(along0(partner, me_t, sendy_sem, recvy_sem))
    peers1 = (near, partner, across)
    out1 = [along1(near, me_t, recv1_sem), along1(partner, me_t, recvp_sem), along1(near, partner, recv1_sem)]
    in_partner = along1(partner, partner, recvp_sem)
    for copy in (over0[7], *out0):
        copy.start()
    load_even.wait()
    for r in range(ROWS1):
        got1[me_t - first, r * SEGS : (r + 1) * SEGS] = field_even[
            pl.ds(r * BLOCK + off1, SEGS, stride=8), :
        ].astype(jnp.bfloat16)
    for copy in (out1[1], out1[0]):
        copy.start()

    def widen(wide, got, slot):
        count = got.shape[1] // SEGS
        for r in range(count):
            wide[pl.ds(slot * count + r, SEGS, stride=M), :] = got[slot, r * SEGS : (r + 1) * SEGS].astype(jnp.float32)

    def pass0(i):
        in0[i].wait_recv()
        over0[i].start()
        widen(wide0, got0, 2 * turn[i] + h)

    load_odd.wait()

    def part_columns(c, carry):
        cols = pl.ds(pl.multiple_of(c * LANES, LANES), LANES)
        at = pl.multiple_of(c * 8, 8)
        for p in range(TILES // 2):
            pair = jnp.concatenate(
                [field_even[pl.ds(p * BLOCK + at, 8), :], field_odd[pl.ds(p * BLOCK + at, 8), :]], axis=0
            )
            rows[16 * p : 16 * (p + 1), cols] = pair.astype(jnp.bfloat16)
        x2 = jnp.concatenate(
            [
                half[pl.ds(at + off2 + more, TILES // 2, stride=BLOCK), :]
                for half in (field_even, field_odd)
                for more in (0, 4)
            ],
            axis=0,
        )
        high2 = x2.astype(jnp.bfloat16)
        rows[X2 : X2 + M, cols] = high2
        rows[X2 + M :, cols] = (x2 - high2.astype(jnp.float32)).astype(jnp.bfloat16)
        return carry

    lax.fori_loop(0, SEGS, part_columns, 0)
    widen(wide0, got0, me_t)
    widen(wide1, got1, me_t - first)

    for fetch in fetches:
        fetch.wait()
    none = lambda count: [jnp.full((1, R), -1, jnp.int32)] * count
    row_m = lax.broadcasted_iota(jnp.int32, (M, LANES), 0)
    for level, (q, place, at) in enumerate(((0, 3, 0), (q1, 2, M), (q2, 0, 2 * M))):
        spots = jnp.concatenate([*none(place), picks[pl.ds(q, 1), :], *none(3 - place)], axis=1)
        columns = exact(basis[level], (row_m == spots).astype(jnp.float32))
        if level == 2:
            pad[...] = columns
            columns = jnp.concatenate([pad[pl.ds(i, M // 4, stride=4), :] for i in range(4)], axis=0)
            chosen[3 * M :] = columns
        chosen[at : at + M] = columns
    turned[...] = chosen[...].T
    at_row = lax.broadcasted_iota(jnp.int32, (STEPS, M), 0)
    order = lax.broadcasted_iota(jnp.int32, (STEPS, M), 1)
    rank = lax.rem(order, M // 4) * 4 + order // (M // 4)
    among[...] = exact((at_row == 4 * rank + off2).astype(jnp.float32), chosen[2 * M : 3 * M])
    def put(ref, tiles):
        for g in range(tiles[0].shape[0] // 8):
            for t in range(2):
                ref[2 * g + t] = tiles[t][8 * g : 8 * (g + 1)]

    space = jnp.zeros((R, 2 * LANES - STEPS), jnp.float32)
    by_field2 = exact(turned[:R, 2 * M :], dot_nt(rows[:STEPS], rows[X2:]), ((1,), (1,)))
    put(part2, [by_field2[:, :LANES], jnp.concatenate([by_field2[:, LANES:], space], axis=1)])

    def others(do):
        pl.when(me_s < OWNERS2)(lambda: do(OWNERS2 - 1))
        pl.when(me_s >= OWNERS2)(lambda: do(OWNERS2))

    for d in range(1, NS):
        tgt = lax.rem(me_s + d, NS)
        copy = pltpu.make_async_remote_copy(
            src_ref=part2.at[lax.rem(tgt, OWNERS2)], dst_ref=inbox2.at[me_s],
            send_sem=sems2[0], recv_sem=sems2[1],
            device_id={"space": tgt}, device_id_type=MESH,
        )
        pl.when(tgt < OWNERS2)(copy.start)

    for i in range(7):
        pass0(i)
        if i == 3:
            in_partner.wait_recv()
            out1[2].start()

    @pl.when(me_s < OWNERS2)
    def _():
        own = lax.rem(me_s, OWNERS2)
        whole(inbox2, NS - 1, sems2[0], sems2[1]).wait_recv()
        acc = part2[own]
        for d in range(1, NS):
            acc = acc + inbox2[lax.rem(me_s + d, NS)]
        total2[own] = acc
        for d in range(1, NS):
            pltpu.make_async_remote_copy(
                src_ref=total2.at[own], dst_ref=total2.at[own], send_sem=sems2[2], recv_sem=sems2[3],
                device_id={"space": lax.rem(me_s + d, NS)}, device_id_type=MESH,
            ).start()

    def unpack(wide, at):
        for j in range(SEGS):
            rows[at : at + M, j * LANES : (j + 1) * LANES] = wide[j * M : (j + 1) * M].astype(jnp.bfloat16)

    whole(got1, 2, send1_sem, recv1_sem).wait_recv()
    for peer in peers1:
        widen(wide1, got1, peer - first)
    unpack(wide1, X1)
    whole(got0, NZ, sendy_sem, recvy_sem).wait_recv()
    for zz in (*turn, z):
        widen(wide0, got0, 2 * zz + 1 - h)
    unpack(wide0, X0)

    samples = rows[X0:X2]
    by_field = dot_nt(samples, rows[:STEPS])
    by_modes = exact(dot_nt(samples, samples), chosen[: 2 * M])
    ends = jnp.concatenate([by_field[:, LANES:], by_modes[:, LANE1:]], axis=1)
    both = exact(turned[LANE1:, : 2 * M], jnp.concatenate([by_field[:, :LANES], ends], axis=1))
    put(part01, [both[:, :LANES], both[:, LANES:]])

    core = lax.rem(me_s, 2)
    chip = me_s // 2
    mate = me_s + 1 - 2 * core
    mine = pl.ds(core * 8, 8)

    def to_mate(src, dst, sems):
        return pltpu.make_async_remote_copy(
            src_ref=src, dst_ref=dst, send_sem=sems[0], recv_sem=sems[1],
            device_id={"space": mate}, device_id_type=MESH,
        )

    give = to_mate(part01.at[pl.ds(8 - core * 8, 8)], inbox_mate, mate_sems)
    give.start()
    give.wait_recv()
    halves[chip] = part01[mine] + inbox_mate[...]
    for d in range(1, CHIPS):
        pltpu.make_async_remote_copy(
            src_ref=halves.at[chip], dst_ref=halves.at[chip], send_sem=chip_sems[0], recv_sem=chip_sems[1],
            device_id={"space": 2 * lax.rem(chip + d, CHIPS) + core}, device_id_type=MESH,
        ).start()
    whole(halves, CHIPS - 1, chip_sems[0], chip_sems[1]).wait_recv()
    acc = halves[0]
    for i in range(1, CHIPS):
        acc = acc + halves[i]
    total01[mine] = acc
    back = to_mate(total01.at[mine], total01.at[mine], back_sems)
    back.start()
    others(lambda count: whole(total2, count, sems2[2], sems2[3]).wait_recv())
    sums[16:] = total2[...]
    back.wait_recv()
    sums[:16] = total01[...]

    whole(got0, NZ - 1, send0_sem, recv0_sem.at[z]).wait_send()
    whole(got0, NZ, sendy_sem, recvy_sem).wait_send()
    whole(got1, GROUP - 1, send1_sem, recv1_sem).wait_send()
    others(lambda count: whole(inbox2, count, sems2[0], sems2[1]).wait_send())
    pl.when(me_s < OWNERS2)(whole(inbox2, NS - 1, sems2[2], sems2[3]).wait_send)
    give.wait_send()
    whole(halves, CHIPS - 1, chip_sems[0], chip_sems[1]).wait_send()
    back.wait_send()


def eliminate(tiles, pivot_tile, pivot_lane):
    sub = lax.broadcasted_iota(jnp.int32, (8, LANES), 0)
    over = lambda x, i: jnp.broadcast_to(x[i : i + 1], (8, LANES))
    count = len(tiles[0])
    ahead = {}
    for k in range(0, R, 2):
        g, i = divmod(k, 8)
        for j in range(k, min(k + 2 * AHEAD + 2, R)):
            if j not in ahead:
                lane = pivot_lane + j
                ahead[j] = [jnp.broadcast_to(row[pivot_tile][:, lane : lane + 1], (8, LANES)) for row in tiles]
        left, right = ahead.pop(k), ahead.pop(k + 1)
        a, b, c, d = over(left[g], i), over(right[g], i), over(left[g], i + 1), over(right[g], i + 1)
        scale = 1.0 / (a * d - b * c)
        a, b, c, d = a * scale, b * scale, c * scale, d * scale

        def pivot(old):
            first, second = over(old[g], i), over(old[g], i + 1)
            upper, lower = d * first - b * second, a * second - c * first
            moved = [old[q] - (left[q] * upper + right[q] * lower) for q in range(len(old))]
            moved[g] = jnp.where(sub == i, upper, jnp.where(sub == i + 1, lower, moved[g]))
            return moved

        ahead = {j: pivot(old) for j, old in ahead.items()}
        columns = [pivot([row[t] for row in tiles]) for t in range(count)]
        tiles = [[columns[t][q] for t in range(count)] for q in range(R // 8)]
    return tiles


def solve(block, pivot):
    tile, at = divmod(pivot, LANES)
    sub = lax.broadcasted_iota(jnp.int32, (8, LANES), 0)
    lane = lax.broadcasted_iota(jnp.int32, (8, LANES), 1)
    tiles = [
        [block[8 * g : 8 * (g + 1), LANES * t : LANES * (t + 1)] for t in range(block.shape[1] // LANES)]
        for g in range(R // 8)
    ]
    for g in range(R // 8):
        tiles[g][tile] = jnp.where(lane == at + 8 * g + sub, tiles[g][tile] + EPS, tiles[g][tile])
    done = eliminate(tiles, tile, at)
    return jnp.concatenate([jnp.concatenate(row, axis=1) for row in done], axis=0)


def update(sums, chosen, among, rows, record, out_hbm, field, out, weights, held, done, early, last, load_sem, store_sem):
    live = lax.axis_index("tm") >= 0
    at1, at0, at2 = LANES + LANE1, LANES + LANE0, 2 * LANES

    load = pltpu.make_async_copy(record, field, load_sem)
    load.start()
    @pl.when(live)
    def _():
        scale = 1.0 / (POINTS * NS)
        tall = lambda first, t: jnp.concatenate([sums[first + 2 * g + t] for g in range(R // 8)], axis=0) * scale
        blocks = []
        for first in (8, 0, 16):
            left, right = tall(first, 0), tall(first, 1)
            by_field = jnp.concatenate([left, right], axis=1)[:, :STEPS]
            blocks.append(jnp.concatenate([left, right, exact(by_field, among[...])], axis=1))
        for level in range(3):
            held[level] = blocks[level]
        done[0] = solve(blocks[0], at0)

    def change(block, done, at):
        cols = slice(at, at + R)
        return exact(block[:, cols] + EPS * done[:, cols], done, ((0,), (0,)))

    @pl.when(live)
    def _():
        held[1] = held[1] - change(held[0], done[0], at1)

    @pl.when(live)
    def _():
        held[2] = held[2] - change(held[0], done[0], at2)
        done[1] = solve(held[1], at1)

    @pl.when(live)
    def _():
        held[2] = held[2] - change(held[1], done[1], at2)

    @pl.when(live)
    def _():
        pick0 = chosen[:M, LANE0 : LANE0 + R]
        pick1 = chosen[M : 2 * M, LANE1 : LANE1 + R]
        done0, done1 = done[0], done[1]
        way1 = -exact(pick0, done0[:, at1 : at1 + R])
        way2 = -exact(pick0, done0[:, at2 : at2 + R]) - exact(way1, done1[:, at2 : at2 + R])
        low2 = -exact(pick1, done1[:, at2 : at2 + R])
        part0 = exact(done0[:, :STEPS], pick0, ((0,), (1,))) + exact(done1[:, :STEPS], way1, ((0,), (1,)))
        part1 = exact(done1[:, :STEPS], pick1, ((0,), (1,)))
        last[: 2 * M] = jnp.concatenate([way2, low2], axis=0)
        last[2 * M :] = chosen[2 * M :, :R]
        early[:, : 2 * M] = jnp.concatenate([part0, part1], axis=1)
        early[:, 2 * M :] = jnp.zeros((STEPS, 2 * M), jnp.float32)
        done[2] = solve(held[2], at2)

    @pl.when(live)
    def _():
        slopes = early[...] + exact(done[2][:, :STEPS], last[...], ((0,), (1,)))
        high = slopes.astype(jnp.bfloat16)
        weights[:STEPS] = high
        weights[STEPS:] = (slopes - high.astype(jnp.float32)).astype(jnp.bfloat16)

    load.wait()
    stores = []
    for c in range(POINTS // WIDTH):
        cols = slice(c * WIDTH, (c + 1) * WIDTH)
        slow = jnp.dot(weights[...], rows[X0:, cols], preferred_element_type=jnp.float32)
        out[:, cols] = field[:, cols] - (slow[:STEPS] + slow[STEPS:])
        store = pltpu.make_async_copy(out.at[:, cols], out_hbm.at[:, cols], store_sem.at[c])
        store.start()
        stores.append(store)
    for store in stores:
        store.wait()


def body(record, mode_basis, slow_picks, phases):
    dma = pltpu.SemaphoreType.DMA
    vmem = pl.BlockSpec(memory_space=pltpu.VMEM)
    hbm = pl.BlockSpec(memory_space=pltpu.MemorySpace.HBM)
    tiled = record.reshape(TILES, 8, SEGS, LANES).transpose(0, 2, 1, 3).reshape(ROWS0, ROWS1 // ROWS0, 2, BLOCK, LANES)
    far = lambda x: pltpu.with_memory_space_constraint(x, pltpu.MemorySpace.HBM)
    chunk = lambda *count: pltpu.VMEM((*count, 8, LANES), jnp.float32)
    rows, sums, chosen, among = pl.pallas_call(
        collect,
        out_shape=[
            pltpu.VMEM((ALL, POINTS), jnp.bfloat16),
            pltpu.VMEM((24, 8, LANES), jnp.float32),
            pltpu.VMEM((4 * M, LANES), jnp.float32),
            pltpu.VMEM((STEPS, LANES), jnp.float32),
        ],
        in_specs=[hbm] * 4,
        out_specs=[vmem] * 4,
        scratch_shapes=[
            pltpu.SMEM((21,), jnp.int32),
            pltpu.VMEM((21, R), jnp.int32),
            pltpu.VMEM((ROWS0 * BLOCK, LANES), jnp.float32),
            pltpu.VMEM((TILES // 2 * BLOCK, LANES), jnp.float32),
            pltpu.VMEM((TILES // 2 * BLOCK, LANES), jnp.float32),
            pltpu.VMEM((NT, ROWS0 * SEGS, LANES), jnp.bfloat16),
            pltpu.VMEM((GROUP, ROWS1 * SEGS, LANES), jnp.bfloat16),
            pltpu.VMEM((M * SEGS, LANES), jnp.float32),
            pltpu.VMEM((M * SEGS, LANES), jnp.float32),
            pltpu.VMEM((3, M, M), jnp.float32),
            pltpu.VMEM((LANES, 4 * M), jnp.float32),
            pltpu.VMEM((M, LANES), jnp.float32),
            chunk(8), chunk(NS), chunk(8), chunk(16), chunk(8), chunk(CHIPS, 8), chunk(16),
            dma((3,)), dma((5,)), dma((NZ,)), dma((16,)),
        ],
        compiler_params=pltpu.CompilerParams(
            collective_id=0, has_side_effects=True, vmem_limit_bytes=VMEM_LIMIT
        ),
        name="collect",
    )(far(phases), far(slow_picks), far(mode_basis), far(tiled))
    near = lambda x: pltpu.with_memory_space_constraint(x, pltpu.VMEM)
    return pl.pallas_call(
        update,
        out_shape=jax.ShapeDtypeStruct((STEPS, POINTS), jnp.float32),
        in_specs=[vmem, vmem, vmem, vmem, hbm],
        out_specs=hbm,
        scratch_shapes=[
            pltpu.VMEM((STEPS, POINTS), jnp.float32),
            pltpu.VMEM((STEPS, POINTS), jnp.float32),
            pltpu.VMEM((2 * STEPS, 4 * M), jnp.bfloat16),
            pltpu.VMEM((3, R, 3 * LANES), jnp.float32),
            pltpu.VMEM((3, R, 3 * LANES), jnp.float32),
            pltpu.VMEM((STEPS, 4 * M), jnp.float32),
            pltpu.VMEM((4 * M, R), jnp.float32),
            dma(()), dma((POINTS // WIDTH,)),
        ],
        compiler_params=pltpu.CompilerParams(vmem_limit_bytes=VMEM_LIMIT),
        name="update",
    )(near(sums), near(chosen), near(among), near(rows), far(record))


def solution(mesh):
    in_specs = (P("tm", "space"), P(), P(), P())
    return jax.shard_map(body, mesh=mesh, in_specs=in_specs, out_specs=P("tm", "space"), check_vma=False)
```

```python
import jax
import jax.numpy as jnp
from jax import lax
from jax.experimental import pallas as pl
from jax.experimental.pallas import tpu as pltpu
from jax.sharding import PartitionSpec as P

M = 48
R = 32
LANES = 128
WIDTH = 512
EPS = 1e-5
AHEAD = 4
MESH = pl.DeviceIdType.MESH
EXACT = lax.Precision.HIGHEST
VMEM_LIMIT = 24 * 1024 * 1024
NT = 16
NS = 16
NZ = NT // 2
CHIPS = NS // 2
GROUP = 4
STEPS = 192
POINTS = 4096
SEGS = POINTS // LANES
TILES = STEPS // 8
BLOCK = SEGS * 8
ROWS0 = M // NT
ROWS1 = M // GROUP
X0 = STEPS
X1 = X0 + M
X2 = X1 + M
ALL = X2 + 2 * M
LANE1 = 64
LANE0 = 96


def dot_nt(a, b):
    return lax.dot_general(a, b, (((1,), (1,)), ((), ())), preferred_element_type=jnp.float32)


def exact(a, b, dims=((1,), (0,))):
    return lax.dot_general(a, b, (dims, ((), ())), precision=EXACT, preferred_element_type=jnp.float32)


def collect(
    phases_hbm, picks_hbm, basis_hbm, record,
    rows, sums, chosen, among,
    phases, picks, head, field_even, field_odd, got0, got1, wide0, wide1, basis, turned, pad,
    part2, inbox2, halves2, total2, part01, inbox01, halves01, total01,
    load_sem, small_sem, recv0_sem, sem,
):
    send0_sem, sendy_sem, recvy_sem, send1_sem, recv1_sem = [sem.at[i] for i in range(5)]
    sems2, sems01 = [[sem.at[i] for i in range(j, j + 6)] for j in (5, 11)]
    recvp_sem, late_sem = sem.at[17], sem.at[18]
    me_t = lax.axis_index("tm")
    me_s = lax.axis_index("space")
    core = lax.rem(me_s, 2)
    first = me_t // GROUP * GROUP

    barrier = pltpu.get_barrier_semaphore()
    for d in range(2, NT, 2):
        pl.semaphore_signal(barrier, inc=1, device_id={"tm": lax.rem(me_t + d, NT)}, device_id_type=MESH)
    partner = me_t + 1 - 2 * lax.rem(me_t, 2)
    pl.semaphore_signal(barrier, inc=1, device_id={"tm": partner}, device_id_type=MESH)
    chip = me_s // 2
    mate = me_s + 1 - 2 * core
    for d in range(1, CHIPS):
        peer = 2 * lax.rem(chip + d, CHIPS) + core
        pl.semaphore_signal(barrier, inc=1, device_id={"space": peer}, device_id_type=MESH)
    pl.semaphore_signal(barrier, inc=1, device_id={"space": mate}, device_id_type=MESH)

    get_phases = pltpu.make_async_copy(phases_hbm, phases, small_sem.at[3])
    get_phases.start()
    load_even, load_odd = [
        pltpu.make_async_copy(record.at[:, :, i], half.reshape(ROWS0, ROWS1 // ROWS0, BLOCK, LANES), load_sem.at[i])
        for i, half in enumerate((field_even, field_odd))
    ]
    load_head = pltpu.make_async_copy(record.at[:, 0, 0], head.reshape(ROWS0, BLOCK, LANES), load_sem.at[2])
    load_head.start()
    load_even.start()
    q1 = 1 + me_t // GROUP
    q2 = 5 + me_t
    fetches = [
        pltpu.make_async_copy(basis_hbm.at[q], basis.at[level], small_sem.at[level])
        for level, q in enumerate((0, q1, q2))
    ]
    fetches.append(pltpu.make_async_copy(picks_hbm, picks, small_sem.at[4]))
    for fetch in fetches:
        fetch.start()
    load_odd.start()

    get_phases.wait()
    off0 = lax.rem(phases[0], STEPS * NT // M)
    off1 = lax.rem(phases[q1], STEPS * GROUP // M)
    off2 = lax.rem(phases[q2], STEPS // M)
    load_head.wait()
    for r in range(ROWS0):
        got0[me_t, r * SEGS : (r + 1) * SEGS] = head[pl.ds(r * BLOCK + off0, SEGS, stride=8), :].astype(jnp.bfloat16)

    pl.semaphore_wait(barrier, NZ + CHIPS)

    z = me_t // 2
    h = lax.rem(me_t, 2)
    near = me_t + 2 - 4 * lax.rem(z, 2)
    across = near + 1 - 2 * h

    def along0(target, owner, send_sem, recv_sem):
        return pltpu.make_async_remote_copy(
            src_ref=got0.at[owner], dst_ref=got0.at[owner], send_sem=send_sem, recv_sem=recv_sem,
            device_id={"tm": target}, device_id_type=MESH,
        )

    def along1(target, owner, recv_sem):
        return pltpu.make_async_remote_copy(
            src_ref=got1.at[owner - first], dst_ref=got1.at[owner - first],
            send_sem=send1_sem, recv_sem=recv_sem,
            device_id={"tm": target}, device_id_type=MESH,
        )

    def whole(ref, count, send_sem, recv_sem):
        place = ref.at[pl.ds(0, count)]
        return pltpu.make_async_remote_copy(
            src_ref=place, dst_ref=place, send_sem=send_sem, recv_sem=recv_sem,
            device_id={"tm": partner}, device_id_type=MESH,
        )

    hops = (1, -1, 2, -2, 3, -3, 4)
    turn = [lax.rem(z + d + NZ, NZ) for d in hops]
    out0 = [along0(2 * turn[i] + h, me_t, send0_sem, recv0_sem.at[z]) for i in range(7)]
    in0 = [along0(2 * turn[i] + h, 2 * turn[i] + h, send0_sem, recv0_sem.at[turn[i]]) for i in range(7)]
    over0 = [along0(partner, 2 * turn[i] + h, sendy_sem, recvy_sem if i < 4 else late_sem) for i in range(7)]
    over0.append(along0(partner, me_t, sendy_sem, recvy_sem))
    peers1 = (near, partner, across)
    out1 = [along1(near, me_t, recv1_sem), along1(partner, me_t, recvp_sem), along1(near, partner, recv1_sem)]
    in_partner = along1(partner, partner, recvp_sem)
    for copy in (over0[7], *out0):
        copy.start()
    load_even.wait()
    for r in range(ROWS1):
        got1[me_t - first, r * SEGS : (r + 1) * SEGS] = field_even[
            pl.ds(r * BLOCK + off1, SEGS, stride=8), :
        ].astype(jnp.bfloat16)
    for copy in (out1[1], out1[0]):
        copy.start()

    def widen(wide, got, slot):
        count = got.shape[1] // SEGS
        for r in range(count):
            wide[pl.ds(slot * count + r, SEGS, stride=M), :] = got[slot, r * SEGS : (r + 1) * SEGS].astype(jnp.float32)

    def pass0(i):
        in0[i].wait_recv()
        over0[i].start()
        widen(wide0, got0, 2 * turn[i] + h)

    load_odd.wait()

    def part_columns(c, carry):
        cols = pl.ds(pl.multiple_of(c * LANES, LANES), LANES)
        at = pl.multiple_of(c * 8, 8)
        for p in range(TILES // 2):
            pair = jnp.concatenate(
                [field_even[pl.ds(p * BLOCK + at, 8), :], field_odd[pl.ds(p * BLOCK + at, 8), :]], axis=0
            )
            rows[16 * p : 16 * (p + 1), cols] = pair.astype(jnp.bfloat16)
        x2 = jnp.concatenate(
            [
                half[pl.ds(at + off2 + more, TILES // 2, stride=BLOCK), :]
                for half in (field_even, field_odd)
                for more in (0, 4)
            ],
            axis=0,
        )
        high2 = x2.astype(jnp.bfloat16)
        rows[X2 : X2 + M, cols] = high2
        rows[X2 + M :, cols] = (x2 - high2.astype(jnp.float32)).astype(jnp.bfloat16)
        return carry

    lax.fori_loop(0, SEGS, part_columns, 0)
    widen(wide0, got0, me_t)
    widen(wide1, got1, me_t - first)

    for fetch in fetches:
        fetch.wait()
    none = lambda count: [jnp.full((1, R), -1, jnp.int32)] * count
    row_m = lax.broadcasted_iota(jnp.int32, (M, LANES), 0)
    for level, (q, place, at) in enumerate(((0, 3, 0), (q1, 2, M), (q2, 0, 2 * M))):
        spots = jnp.concatenate([*none(place), picks[pl.ds(q, 1), :], *none(3 - place)], axis=1)
        columns = exact(basis[level], (row_m == spots).astype(jnp.float32))
        if level == 2:
            pad[...] = columns
            columns = jnp.concatenate([pad[pl.ds(i, M // 4, stride=4), :] for i in range(4)], axis=0)
            chosen[3 * M :] = columns
        chosen[at : at + M] = columns
    turned[...] = chosen[...].T
    at_row = lax.broadcasted_iota(jnp.int32, (STEPS, M), 0)
    order = lax.broadcasted_iota(jnp.int32, (STEPS, M), 1)
    rank = lax.rem(order, M // 4) * 4 + order // (M // 4)
    among[...] = exact((at_row == 4 * rank + off2).astype(jnp.float32), chosen[2 * M : 3 * M])
    def put(ref, tiles):
        for g in range(tiles[0].shape[0] // 8):
            for t in range(2):
                ref[2 * g + t] = tiles[t][8 * g : 8 * (g + 1)]

    space = jnp.zeros((R, 2 * LANES - STEPS), jnp.float32)
    by_field2 = exact(turned[:R, 2 * M :], dot_nt(rows[:STEPS], rows[X2:]), ((1,), (1,)))
    put(part2, [by_field2[:, :LANES], jnp.concatenate([by_field2[:, LANES:], space], axis=1)])

    def to_mate(src, dst, sems):
        return pltpu.make_async_remote_copy(
            src_ref=src, dst_ref=dst, send_sem=sems[0], recv_sem=sems[1],
            device_id={"space": mate}, device_id_type=MESH,
        )

    class Sum:
        def __init__(self, part, inbox, halves, total, sems):
            self.part, self.inbox, self.halves, self.total, self.sems = part, inbox, halves, total, sems
            count = inbox.shape[0]
            self.mine = pl.ds(core * count, count)
            self.give = to_mate(part.at[pl.ds(count - core * count, count)], inbox, sems[:2])
            self.back = to_mate(total.at[self.mine], total.at[self.mine], sems[4:])

        def swap(self):
            self.give.wait_recv()
            self.halves[chip] = self.part[self.mine] + self.inbox[...]
            for d in range(1, CHIPS):
                pltpu.make_async_remote_copy(
                    src_ref=self.halves.at[chip], dst_ref=self.halves.at[chip],
                    send_sem=self.sems[2], recv_sem=self.sems[3],
                    device_id={"space": 2 * lax.rem(chip + d, CHIPS) + core}, device_id_type=MESH,
                ).start()

        def add(self):
            self.swapped().wait_recv()
            acc = self.halves[0]
            for i in range(1, CHIPS):
                acc = acc + self.halves[i]
            self.total[self.mine] = acc
            self.back.start()

        def swapped(self):
            return whole(self.halves, CHIPS - 1, self.sems[2], self.sems[3])

        def settle(self):
            self.give.wait_send()
            self.swapped().wait_send()
            self.back.wait_send()

    sum2 = Sum(part2, inbox2, halves2, total2, sems2)
    sum01 = Sum(part01, inbox01, halves01, total01, sems01)
    sum2.give.start()

    for i in range(7):
        pass0(i)
        if i == 3:
            in_partner.wait_recv()
            out1[2].start()

    sum2.swap()

    def unpack(wide, at):
        for j in range(SEGS):
            rows[at : at + M, j * LANES : (j + 1) * LANES] = wide[j * M : (j + 1) * M].astype(jnp.bfloat16)

    whole(got1, 2, send1_sem, recv1_sem).wait_recv()
    for peer in peers1:
        widen(wide1, got1, peer - first)
    unpack(wide1, X1)
    whole(got0, 5, sendy_sem, recvy_sem).wait_recv()
    for zz in (*turn[:4], z):
        widen(wide0, got0, 2 * zz + 1 - h)
    whole(got0, 3, sendy_sem, late_sem).wait_recv()
    for zz in turn[4:]:
        widen(wide0, got0, 2 * zz + 1 - h)
    unpack(wide0, X0)

    samples = rows[X0:X2]
    by_field = dot_nt(samples, rows[:STEPS])
    by_modes = exact(dot_nt(samples, samples), chosen[: 2 * M])
    ends = jnp.concatenate([by_field[:, LANES:], by_modes[:, LANE1:]], axis=1)
    both = exact(turned[LANE1:, : 2 * M], jnp.concatenate([by_field[:, :LANES], ends], axis=1))
    put(part01, [both[:, :LANES], both[:, LANES:]])

    sum01.give.start()
    sum2.add()
    sum01.swap()
    sum01.add()
    sum2.back.wait_recv()
    sums[16:] = total2[...]
    sum01.back.wait_recv()
    sums[:16] = total01[...]

    whole(got0, NZ - 1, send0_sem, recv0_sem.at[z]).wait_send()
    whole(got0, NZ, sendy_sem, recvy_sem).wait_send()
    whole(got1, GROUP - 1, send1_sem, recv1_sem).wait_send()
    sum2.settle()
    sum01.settle()


def eliminate(tiles, pivot_tile, pivot_lane):
    sub = lax.broadcasted_iota(jnp.int32, (8, LANES), 0)
    over = lambda x, i: jnp.broadcast_to(x[i : i + 1], (8, LANES))
    count = len(tiles[0])
    ahead = {}
    for k in range(0, R, 2):
        g, i = divmod(k, 8)
        for j in range(k, min(k + 2 * AHEAD + 2, R)):
            if j not in ahead:
                lane = pivot_lane + j
                ahead[j] = [jnp.broadcast_to(row[pivot_tile][:, lane : lane + 1], (8, LANES)) for row in tiles]
        left, right = ahead.pop(k), ahead.pop(k + 1)
        a, b, c, d = over(left[g], i), over(right[g], i), over(left[g], i + 1), over(right[g], i + 1)
        scale = 1.0 / (a * d - b * c)
        a, b, c, d = a * scale, b * scale, c * scale, d * scale

        def pivot(old):
            first, second = over(old[g], i), over(old[g], i + 1)
            upper, lower = d * first - b * second, a * second - c * first
            moved = [old[q] - (left[q] * upper + right[q] * lower) for q in range(len(old))]
            moved[g] = jnp.where(sub == i, upper, jnp.where(sub == i + 1, lower, moved[g]))
            return moved

        ahead = {j: pivot(old) for j, old in ahead.items()}
        columns = [pivot([row[t] for row in tiles]) for t in range(count)]
        tiles = [[columns[t][q] for t in range(count)] for q in range(R // 8)]
    return tiles


def solve(block, pivot):
    tile, at = divmod(pivot, LANES)
    sub = lax.broadcasted_iota(jnp.int32, (8, LANES), 0)
    lane = lax.broadcasted_iota(jnp.int32, (8, LANES), 1)
    tiles = [
        [block[8 * g : 8 * (g + 1), LANES * t : LANES * (t + 1)] for t in range(block.shape[1] // LANES)]
        for g in range(R // 8)
    ]
    for g in range(R // 8):
        tiles[g][tile] = jnp.where(lane == at + 8 * g + sub, tiles[g][tile] + EPS, tiles[g][tile])
    done = eliminate(tiles, tile, at)
    return jnp.concatenate([jnp.concatenate(row, axis=1) for row in done], axis=0)


def update(sums, chosen, among, rows, record, out_hbm, field, out, weights, held, done, early, last, load_sem, store_sem):
    live = lax.axis_index("tm") >= 0
    at1, at0, at2 = LANES + LANE1, LANES + LANE0, 2 * LANES

    load = pltpu.make_async_copy(record, field, load_sem)
    load.start()
    @pl.when(live)
    def _():
        scale = 1.0 / (POINTS * NS)
        tall = lambda first, t: jnp.concatenate([sums[first + 2 * g + t] for g in range(R // 8)], axis=0) * scale
        blocks = []
        for first in (8, 0, 16):
            left, right = tall(first, 0), tall(first, 1)
            by_field = jnp.concatenate([left, right], axis=1)[:, :STEPS]
            blocks.append(jnp.concatenate([left, right, exact(by_field, among[...])], axis=1))
        for level in range(3):
            held[level] = blocks[level]
        done[0] = solve(blocks[0], at0)

    def change(block, done, at):
        cols = slice(at, at + R)
        return exact(block[:, cols] + EPS * done[:, cols], done, ((0,), (0,)))

    @pl.when(live)
    def _():
        held[1] = held[1] - change(held[0], done[0], at1)

    @pl.when(live)
    def _():
        held[2] = held[2] - change(held[0], done[0], at2)
        pick0 = chosen[:M, LANE0 : LANE0 + R]
        done0 = done[0]
        way1 = -exact(pick0, done0[:, at1 : at1 + R])
        last[M : 2 * M] = way1
        last[:M] = -exact(pick0, done0[:, at2 : at2 + R])
        early[:, :M] = exact(done0[:, :STEPS], pick0, ((0,), (1,)))
        early[:, 2 * M :] = jnp.zeros((STEPS, 2 * M), jnp.float32)
        done[1] = solve(held[1], at1)

    @pl.when(live)
    def _():
        held[2] = held[2] - change(held[1], done[1], at2)

    @pl.when(live)
    def _():
        pick1 = chosen[M : 2 * M, LANE1 : LANE1 + R]
        done1 = done[1]
        way1 = last[M : 2 * M]
        by_field1 = done1[:, :STEPS]
        early[:, :M] = early[:, :M] + exact(by_field1, way1, ((0,), (1,)))
        early[:, M : 2 * M] = exact(by_field1, pick1, ((0,), (1,)))
        last[:M] = last[:M] - exact(way1, done1[:, at2 : at2 + R])
        last[M : 2 * M] = -exact(pick1, done1[:, at2 : at2 + R])
        last[2 * M :] = chosen[2 * M :, :R]
        done[2] = solve(held[2], at2)

    @pl.when(live)
    def _():
        slopes = early[...] + exact(done[2][:, :STEPS], last[...], ((0,), (1,)))
        high = slopes.astype(jnp.bfloat16)
        weights[:STEPS] = high
        weights[STEPS:] = (slopes - high.astype(jnp.float32)).astype(jnp.bfloat16)

    load.wait()
    stores = []
    for c in range(POINTS // WIDTH):
        cols = slice(c * WIDTH, (c + 1) * WIDTH)
        slow = jnp.dot(weights[...], rows[X0:, cols], preferred_element_type=jnp.float32)
        out[:, cols] = field[:, cols] - (slow[:STEPS] + slow[STEPS:])
        store = pltpu.make_async_copy(out.at[:, cols], out_hbm.at[:, cols], store_sem.at[c])
        store.start()
        stores.append(store)
    for store in stores:
        store.wait()


def body(record, mode_basis, slow_picks, phases):
    dma = pltpu.SemaphoreType.DMA
    vmem = pl.BlockSpec(memory_space=pltpu.VMEM)
    hbm = pl.BlockSpec(memory_space=pltpu.MemorySpace.HBM)
    tiled = record.reshape(TILES, 8, SEGS, LANES).transpose(0, 2, 1, 3).reshape(ROWS0, ROWS1 // ROWS0, 2, BLOCK, LANES)
    far = lambda x: pltpu.with_memory_space_constraint(x, pltpu.MemorySpace.HBM)
    chunk = lambda *count: pltpu.VMEM((*count, 8, LANES), jnp.float32)
    rows, sums, chosen, among = pl.pallas_call(
        collect,
        out_shape=[
            pltpu.VMEM((ALL, POINTS), jnp.bfloat16),
            pltpu.VMEM((24, 8, LANES), jnp.float32),
            pltpu.VMEM((4 * M, LANES), jnp.float32),
            pltpu.VMEM((STEPS, LANES), jnp.float32),
        ],
        in_specs=[hbm] * 4,
        out_specs=[vmem] * 4,
        scratch_shapes=[
            pltpu.SMEM((21,), jnp.int32),
            pltpu.VMEM((21, R), jnp.int32),
            pltpu.VMEM((ROWS0 * BLOCK, LANES), jnp.float32),
            pltpu.VMEM((TILES // 2 * BLOCK, LANES), jnp.float32),
            pltpu.VMEM((TILES // 2 * BLOCK, LANES), jnp.float32),
            pltpu.VMEM((NT, ROWS0 * SEGS, LANES), jnp.bfloat16),
            pltpu.VMEM((GROUP, ROWS1 * SEGS, LANES), jnp.bfloat16),
            pltpu.VMEM((M * SEGS, LANES), jnp.float32),
            pltpu.VMEM((M * SEGS, LANES), jnp.float32),
            pltpu.VMEM((3, M, M), jnp.float32),
            pltpu.VMEM((LANES, 4 * M), jnp.float32),
            pltpu.VMEM((M, LANES), jnp.float32),
            chunk(8), chunk(4), chunk(CHIPS, 4), chunk(8), chunk(16), chunk(8), chunk(CHIPS, 8), chunk(16),
            dma((3,)), dma((5,)), dma((NZ,)), dma((19,)),
        ],
        compiler_params=pltpu.CompilerParams(
            collective_id=0, has_side_effects=True, vmem_limit_bytes=VMEM_LIMIT
        ),
        name="collect",
    )(far(phases), far(slow_picks), far(mode_basis), far(tiled))
    near = lambda x: pltpu.with_memory_space_constraint(x, pltpu.VMEM)
    return pl.pallas_call(
        update,
        out_shape=jax.ShapeDtypeStruct((STEPS, POINTS), jnp.float32),
        in_specs=[vmem, vmem, vmem, vmem, hbm],
        out_specs=hbm,
        scratch_shapes=[
            pltpu.VMEM((STEPS, POINTS), jnp.float32),
            pltpu.VMEM((STEPS, POINTS), jnp.float32),
            pltpu.VMEM((2 * STEPS, 4 * M), jnp.bfloat16),
            pltpu.VMEM((3, R, 3 * LANES), jnp.float32),
            pltpu.VMEM((3, R, 3 * LANES), jnp.float32),
            pltpu.VMEM((STEPS, 4 * M), jnp.float32),
            pltpu.VMEM((4 * M, R), jnp.float32),
            dma(()), dma((POINTS // WIDTH,)),
        ],
        compiler_params=pltpu.CompilerParams(vmem_limit_bytes=VMEM_LIMIT),
        name="update",
    )(near(sums), near(chosen), near(among), near(rows), far(record))


def solution(mesh):
    in_specs = (P("tm", "space"), P(), P(), P())
    return jax.shard_map(body, mesh=mesh, in_specs=in_specs, out_specs=P("tm", "space"), check_vma=False)
```

```python
import jax
import jax.numpy as jnp
from jax import lax
from jax.experimental import pallas as pl
from jax.experimental.pallas import tpu as pltpu
from jax.sharding import PartitionSpec as P

M = 48
R = 32
LANES = 128
WIDTH = 512
EPS = 1e-5
AHEAD = 4
MESH = pl.DeviceIdType.MESH
EXACT = lax.Precision.HIGHEST
VMEM_LIMIT = 24 * 1024 * 1024
NT = 16
NS = 16
NZ = NT // 2
CHIPS = NS // 2
GROUP = 4
STEPS = 192
POINTS = 4096
SEGS = POINTS // LANES
TILES = STEPS // 8
BLOCK = SEGS * 8
ROWS0 = M // NT
ROWS1 = M // GROUP
X0 = STEPS
X1 = X0 + M
X2 = X1 + M
ALL = X2 + 2 * M
LANE1 = 64
LANE0 = 96


def dot_nt(a, b):
    return lax.dot_general(a, b, (((1,), (1,)), ((), ())), preferred_element_type=jnp.float32)


def exact(a, b, dims=((1,), (0,))):
    return lax.dot_general(a, b, (dims, ((), ())), precision=EXACT, preferred_element_type=jnp.float32)


def collect(
    phases_hbm, picks_hbm, basis_hbm, record,
    rows, sums, chosen, among,
    phases, picks, head, field_even, field_odd, got0, got1, wide0, wide1, basis, turned, pad,
    part2, inbox2, halves2, total2, part01, inbox01, halves01, total01,
    load_sem, small_sem, recv0_sem, sem,
):
    send0_sem, sendy_sem, recvy_sem, send1_sem, recv1_sem = [sem.at[i] for i in range(5)]
    sems2, sems01 = [[sem.at[i] for i in range(j, j + 6)] for j in (5, 11)]
    recvp_sem, late_sem = sem.at[17], sem.at[18]
    me_t = lax.axis_index("tm")
    me_s = lax.axis_index("space")
    core = lax.rem(me_s, 2)
    first = me_t // GROUP * GROUP

    barrier = pltpu.get_barrier_semaphore()
    for d in range(2, NT, 2):
        pl.semaphore_signal(barrier, inc=1, device_id={"tm": lax.rem(me_t + d, NT)}, device_id_type=MESH)
    partner = me_t + 1 - 2 * lax.rem(me_t, 2)
    pl.semaphore_signal(barrier, inc=1, device_id={"tm": partner}, device_id_type=MESH)
    chip = me_s // 2
    mate = me_s + 1 - 2 * core
    for d in range(1, CHIPS):
        peer = 2 * lax.rem(chip + d, CHIPS) + core
        pl.semaphore_signal(barrier, inc=1, device_id={"space": peer}, device_id_type=MESH)
    pl.semaphore_signal(barrier, inc=1, device_id={"space": mate}, device_id_type=MESH)

    get_phases = pltpu.make_async_copy(phases_hbm, phases, small_sem.at[3])
    get_phases.start()
    load_even, load_odd = [
        pltpu.make_async_copy(record.at[:, :, i], half.reshape(ROWS0, ROWS1 // ROWS0, BLOCK, LANES), load_sem.at[i])
        for i, half in enumerate((field_even, field_odd))
    ]
    load_head = pltpu.make_async_copy(record.at[:, 0, 0], head.reshape(ROWS0, BLOCK, LANES), load_sem.at[2])
    load_head.start()
    load_even.start()
    q1 = 1 + me_t // GROUP
    q2 = 5 + me_t
    fetches = [
        pltpu.make_async_copy(basis_hbm.at[q], basis.at[level], small_sem.at[level])
        for level, q in enumerate((0, q1, q2))
    ]
    fetches.append(pltpu.make_async_copy(picks_hbm, picks, small_sem.at[4]))
    for fetch in fetches:
        fetch.start()
    load_odd.start()

    get_phases.wait()
    off0 = lax.rem(phases[0], STEPS * NT // M)
    off1 = lax.rem(phases[q1], STEPS * GROUP // M)
    off2 = lax.rem(phases[q2], STEPS // M)
    load_head.wait()
    for r in range(ROWS0):
        got0[me_t, r * SEGS : (r + 1) * SEGS] = head[pl.ds(r * BLOCK + off0, SEGS, stride=8), :].astype(jnp.bfloat16)

    pl.semaphore_wait(barrier, NZ + CHIPS)

    z = me_t // 2
    h = lax.rem(me_t, 2)
    near = me_t + 2 - 4 * lax.rem(z, 2)
    across = near + 1 - 2 * h

    def along0(target, owner, send_sem, recv_sem):
        return pltpu.make_async_remote_copy(
            src_ref=got0.at[owner], dst_ref=got0.at[owner], send_sem=send_sem, recv_sem=recv_sem,
            device_id={"tm": target}, device_id_type=MESH,
        )

    def along1(target, owner, recv_sem):
        return pltpu.make_async_remote_copy(
            src_ref=got1.at[owner - first], dst_ref=got1.at[owner - first],
            send_sem=send1_sem, recv_sem=recv_sem,
            device_id={"tm": target}, device_id_type=MESH,
        )

    def whole(ref, count, send_sem, recv_sem):
        place = ref.at[pl.ds(0, count)]
        return pltpu.make_async_remote_copy(
            src_ref=place, dst_ref=place, send_sem=send_sem, recv_sem=recv_sem,
            device_id={"tm": partner}, device_id_type=MESH,
        )

    hops = (1, -1, 2, -2, 3, -3, 4)
    turn = [lax.rem(z + d + NZ, NZ) for d in hops]
    out0 = [along0(2 * turn[i] + h, me_t, send0_sem, recv0_sem.at[z]) for i in range(7)]
    in0 = [along0(2 * turn[i] + h, 2 * turn[i] + h, send0_sem, recv0_sem.at[turn[i]]) for i in range(7)]
    over0 = [along0(partner, 2 * turn[i] + h, sendy_sem, recvy_sem if i < 4 else late_sem) for i in range(7)]
    over0.append(along0(partner, me_t, sendy_sem, recvy_sem))
    peers1 = (near, partner, across)
    out1 = [along1(near, me_t, recv1_sem), along1(partner, me_t, recvp_sem), along1(near, partner, recv1_sem)]
    in_partner = along1(partner, partner, recvp_sem)
    for copy in (over0[7], *out0):
        copy.start()
    load_even.wait()
    for r in range(ROWS1):
        got1[me_t - first, r * SEGS : (r + 1) * SEGS] = field_even[
            pl.ds(r * BLOCK + off1, SEGS, stride=8), :
        ].astype(jnp.bfloat16)
    out1[1].start()

    def widen(wide, got, slot):
        count = got.shape[1] // SEGS
        for r in range(count):
            wide[pl.ds(slot * count + r, SEGS, stride=M), :] = got[slot, r * SEGS : (r + 1) * SEGS].astype(jnp.float32)

    def pass0(i):
        in0[i].wait_recv()
        over0[i].start()
        widen(wide0, got0, 2 * turn[i] + h)

    load_odd.wait()

    def part_columns(c, carry):
        cols = pl.ds(pl.multiple_of(c * LANES, LANES), LANES)
        at = pl.multiple_of(c * 8, 8)
        for p in range(TILES // 2):
            pair = jnp.concatenate(
                [field_even[pl.ds(p * BLOCK + at, 8), :], field_odd[pl.ds(p * BLOCK + at, 8), :]], axis=0
            )
            rows[16 * p : 16 * (p + 1), cols] = pair.astype(jnp.bfloat16)
        x2 = jnp.concatenate(
            [
                half[pl.ds(at + off2 + more, TILES // 2, stride=BLOCK), :]
                for half in (field_even, field_odd)
                for more in (0, 4)
            ],
            axis=0,
        )
        high2 = x2.astype(jnp.bfloat16)
        rows[X2 : X2 + M, cols] = high2
        rows[X2 + M :, cols] = (x2 - high2.astype(jnp.float32)).astype(jnp.bfloat16)
        return carry

    lax.fori_loop(0, SEGS, part_columns, 0)
    widen(wide0, got0, me_t)
    widen(wide1, got1, me_t - first)

    for fetch in fetches:
        fetch.wait()
    none = lambda count: [jnp.full((1, R), -1, jnp.int32)] * count
    row_m = lax.broadcasted_iota(jnp.int32, (M, LANES), 0)
    for level, (q, place, at) in enumerate(((0, 3, 0), (q1, 2, M), (q2, 0, 2 * M))):
        spots = jnp.concatenate([*none(place), picks[pl.ds(q, 1), :], *none(3 - place)], axis=1)
        columns = exact(basis[level], (row_m == spots).astype(jnp.float32))
        if level == 2:
            pad[...] = columns
            columns = jnp.concatenate([pad[pl.ds(i, M // 4, stride=4), :] for i in range(4)], axis=0)
            chosen[3 * M :] = columns
        chosen[at : at + M] = columns
    turned[...] = chosen[...].T
    at_row = lax.broadcasted_iota(jnp.int32, (STEPS, M), 0)
    order = lax.broadcasted_iota(jnp.int32, (STEPS, M), 1)
    rank = lax.rem(order, M // 4) * 4 + order // (M // 4)
    among[...] = exact((at_row == 4 * rank + off2).astype(jnp.float32), chosen[2 * M : 3 * M])
    def put(ref, tiles):
        for g in range(tiles[0].shape[0] // 8):
            for t in range(2):
                ref[2 * g + t] = tiles[t][8 * g : 8 * (g + 1)]

    space = jnp.zeros((R, 2 * LANES - STEPS), jnp.float32)
    by_field2 = exact(turned[:R, 2 * M :], dot_nt(rows[:STEPS], rows[X2:]), ((1,), (1,)))
    put(part2, [by_field2[:, :LANES], jnp.concatenate([by_field2[:, LANES:], space], axis=1)])

    def to_mate(src, dst, sems):
        return pltpu.make_async_remote_copy(
            src_ref=src, dst_ref=dst, send_sem=sems[0], recv_sem=sems[1],
            device_id={"space": mate}, device_id_type=MESH,
        )

    class Sum:
        def __init__(self, part, inbox, halves, total, sems):
            self.part, self.inbox, self.halves, self.total, self.sems = part, inbox, halves, total, sems
            count = inbox.shape[0]
            self.mine = pl.ds(core * count, count)
            self.give = to_mate(part.at[pl.ds(count - core * count, count)], inbox, sems[:2])
            self.back = to_mate(total.at[self.mine], total.at[self.mine], sems[4:])

        def swap(self):
            self.give.wait_recv()
            self.halves[chip] = self.part[self.mine] + self.inbox[...]
            for d in range(1, CHIPS):
                pltpu.make_async_remote_copy(
                    src_ref=self.halves.at[chip], dst_ref=self.halves.at[chip],
                    send_sem=self.sems[2], recv_sem=self.sems[3],
                    device_id={"space": 2 * lax.rem(chip + d, CHIPS) + core}, device_id_type=MESH,
                ).start()

        def add(self):
            self.swapped().wait_recv()
            acc = self.halves[0]
            for i in range(1, CHIPS):
                acc = acc + self.halves[i]
            self.total[self.mine] = acc
            self.back.start()

        def swapped(self):
            return whole(self.halves, CHIPS - 1, self.sems[2], self.sems[3])

        def settle(self):
            self.give.wait_send()
            self.swapped().wait_send()
            self.back.wait_send()

    sum2 = Sum(part2, inbox2, halves2, total2, sems2)
    sum01 = Sum(part01, inbox01, halves01, total01, sems01)
    sum2.give.start()

    for i in range(7):
        pass0(i)
        if i == 1:
            out1[0].start()
        if i == 3:
            in_partner.wait_recv()
            out1[2].start()

    sum2.swap()

    def unpack(wide, at):
        for j in range(SEGS):
            rows[at : at + M, j * LANES : (j + 1) * LANES] = wide[j * M : (j + 1) * M].astype(jnp.bfloat16)

    whole(got1, 2, send1_sem, recv1_sem).wait_recv()
    for peer in peers1:
        widen(wide1, got1, peer - first)
    unpack(wide1, X1)
    whole(got0, 5, sendy_sem, recvy_sem).wait_recv()
    for zz in (*turn[:4], z):
        widen(wide0, got0, 2 * zz + 1 - h)
    whole(got0, 3, sendy_sem, late_sem).wait_recv()
    for zz in turn[4:]:
        widen(wide0, got0, 2 * zz + 1 - h)
    unpack(wide0, X0)

    samples = rows[X0:X2]
    by_field = dot_nt(samples, rows[:STEPS])
    by_modes = exact(dot_nt(samples, samples), chosen[: 2 * M])
    ends = jnp.concatenate([by_field[:, LANES:], by_modes[:, LANE1:]], axis=1)
    both = exact(turned[LANE1:, : 2 * M], jnp.concatenate([by_field[:, :LANES], ends], axis=1))
    put(part01, [both[:, :LANES], both[:, LANES:]])

    sum01.give.start()
    sum01.swap()
    sum2.add()
    sum01.add()
    sum2.back.wait_recv()
    sums[16:] = total2[...]
    sum01.back.wait_recv()
    sums[:16] = total01[...]

    whole(got0, NZ - 1, send0_sem, recv0_sem.at[z]).wait_send()
    whole(got0, NZ, sendy_sem, recvy_sem).wait_send()
    whole(got1, GROUP - 1, send1_sem, recv1_sem).wait_send()
    sum2.settle()
    sum01.settle()


def eliminate(tiles, pivot_tile, pivot_lane):
    sub = lax.broadcasted_iota(jnp.int32, (8, LANES), 0)
    over = lambda x, i: jnp.broadcast_to(x[i : i + 1], (8, LANES))
    count = len(tiles[0])
    ahead = {}
    for k in range(0, R, 2):
        g, i = divmod(k, 8)
        for j in range(k, min(k + 2 * AHEAD + 2, R)):
            if j not in ahead:
                lane = pivot_lane + j
                ahead[j] = [jnp.broadcast_to(row[pivot_tile][:, lane : lane + 1], (8, LANES)) for row in tiles]
        left, right = ahead.pop(k), ahead.pop(k + 1)
        a, b, c, d = over(left[g], i), over(right[g], i), over(left[g], i + 1), over(right[g], i + 1)
        scale = 1.0 / (a * d - b * c)
        a, b, c, d = a * scale, b * scale, c * scale, d * scale

        def pivot(old):
            first, second = over(old[g], i), over(old[g], i + 1)
            upper, lower = d * first - b * second, a * second - c * first
            moved = [old[q] - (left[q] * upper + right[q] * lower) for q in range(len(old))]
            moved[g] = jnp.where(sub == i, upper, jnp.where(sub == i + 1, lower, moved[g]))
            return moved

        ahead = {j: pivot(old) for j, old in ahead.items()}
        columns = [pivot([row[t] for row in tiles]) for t in range(count)]
        tiles = [[columns[t][q] for t in range(count)] for q in range(R // 8)]
    return tiles


def solve(block, pivot):
    tile, at = divmod(pivot, LANES)
    sub = lax.broadcasted_iota(jnp.int32, (8, LANES), 0)
    lane = lax.broadcasted_iota(jnp.int32, (8, LANES), 1)
    tiles = [
        [block[8 * g : 8 * (g + 1), LANES * t : LANES * (t + 1)] for t in range(block.shape[1] // LANES)]
        for g in range(R // 8)
    ]
    for g in range(R // 8):
        tiles[g][tile] = jnp.where(lane == at + 8 * g + sub, tiles[g][tile] + EPS, tiles[g][tile])
    done = eliminate(tiles, tile, at)
    return jnp.concatenate([jnp.concatenate(row, axis=1) for row in done], axis=0)


def update(sums, chosen, among, rows, record, out_hbm, field, out, weights, held, done, early, last, load_sem, store_sem):
    live = lax.axis_index("tm") >= 0
    at1, at0, at2 = LANES + LANE1, LANES + LANE0, 2 * LANES

    load = pltpu.make_async_copy(record, field, load_sem)
    load.start()
    @pl.when(live)
    def _():
        scale = 1.0 / (POINTS * NS)
        tall = lambda first, t: jnp.concatenate([sums[first + 2 * g + t] for g in range(R // 8)], axis=0) * scale
        blocks = []
        for first in (8, 0, 16):
            left, right = tall(first, 0), tall(first, 1)
            by_field = jnp.concatenate([left, right], axis=1)[:, :STEPS]
            blocks.append(jnp.concatenate([left, right, exact(by_field, among[...])], axis=1))
        for level in range(3):
            held[level] = blocks[level]
        done[0] = solve(blocks[0], at0)

    def change(block, done, at):
        cols = slice(at, at + R)
        return exact(block[:, cols] + EPS * done[:, cols], done, ((0,), (0,)))

    @pl.when(live)
    def _():
        held[1] = held[1] - change(held[0], done[0], at1)

    @pl.when(live)
    def _():
        held[2] = held[2] - change(held[0], done[0], at2)
        pick0 = chosen[:M, LANE0 : LANE0 + R]
        done0 = done[0]
        way1 = -exact(pick0, done0[:, at1 : at1 + R])
        last[M : 2 * M] = way1
        last[:M] = -exact(pick0, done0[:, at2 : at2 + R])
        early[:, :M] = exact(done0[:, :STEPS], pick0, ((0,), (1,)))
        early[:, 2 * M :] = jnp.zeros((STEPS, 2 * M), jnp.float32)
        done[1] = solve(held[1], at1)

    @pl.when(live)
    def _():
        held[2] = held[2] - change(held[1], done[1], at2)

    @pl.when(live)
    def _():
        pick1 = chosen[M : 2 * M, LANE1 : LANE1 + R]
        done1 = done[1]
        way1 = last[M : 2 * M]
        by_field1 = done1[:, :STEPS]
        early[:, :M] = early[:, :M] + exact(by_field1, way1, ((0,), (1,)))
        early[:, M : 2 * M] = exact(by_field1, pick1, ((0,), (1,)))
        last[:M] = last[:M] - exact(way1, done1[:, at2 : at2 + R])
        last[M : 2 * M] = -exact(pick1, done1[:, at2 : at2 + R])
        last[2 * M :] = chosen[2 * M :, :R]
        done[2] = solve(held[2], at2)

    @pl.when(live)
    def _():
        slopes = early[...] + exact(done[2][:, :STEPS], last[...], ((0,), (1,)))
        high = slopes.astype(jnp.bfloat16)
        weights[:STEPS] = high
        weights[STEPS:] = (slopes - high.astype(jnp.float32)).astype(jnp.bfloat16)

    load.wait()
    stores = []
    for c in range(POINTS // WIDTH):
        cols = slice(c * WIDTH, (c + 1) * WIDTH)
        slow = jnp.dot(weights[...], rows[X0:, cols], preferred_element_type=jnp.float32)
        out[:, cols] = field[:, cols] - (slow[:STEPS] + slow[STEPS:])
        store = pltpu.make_async_copy(out.at[:, cols], out_hbm.at[:, cols], store_sem.at[c])
        store.start()
        stores.append(store)
    for store in stores:
        store.wait()


def body(record, mode_basis, slow_picks, phases):
    dma = pltpu.SemaphoreType.DMA
    vmem = pl.BlockSpec(memory_space=pltpu.VMEM)
    hbm = pl.BlockSpec(memory_space=pltpu.MemorySpace.HBM)
    tiled = record.reshape(TILES, 8, SEGS, LANES).transpose(0, 2, 1, 3).reshape(ROWS0, ROWS1 // ROWS0, 2, BLOCK, LANES)
    far = lambda x: pltpu.with_memory_space_constraint(x, pltpu.MemorySpace.HBM)
    chunk = lambda *count: pltpu.VMEM((*count, 8, LANES), jnp.float32)
    rows, sums, chosen, among = pl.pallas_call(
        collect,
        out_shape=[
            pltpu.VMEM((ALL, POINTS), jnp.bfloat16),
            pltpu.VMEM((24, 8, LANES), jnp.float32),
            pltpu.VMEM((4 * M, LANES), jnp.float32),
            pltpu.VMEM((STEPS, LANES), jnp.float32),
        ],
        in_specs=[hbm] * 4,
        out_specs=[vmem] * 4,
        scratch_shapes=[
            pltpu.SMEM((21,), jnp.int32),
            pltpu.VMEM((21, R), jnp.int32),
            pltpu.VMEM((ROWS0 * BLOCK, LANES), jnp.float32),
            pltpu.VMEM((TILES // 2 * BLOCK, LANES), jnp.float32),
            pltpu.VMEM((TILES // 2 * BLOCK, LANES), jnp.float32),
            pltpu.VMEM((NT, ROWS0 * SEGS, LANES), jnp.bfloat16),
            pltpu.VMEM((GROUP, ROWS1 * SEGS, LANES), jnp.bfloat16),
            pltpu.VMEM((M * SEGS, LANES), jnp.float32),
            pltpu.VMEM((M * SEGS, LANES), jnp.float32),
            pltpu.VMEM((3, M, M), jnp.float32),
            pltpu.VMEM((LANES, 4 * M), jnp.float32),
            pltpu.VMEM((M, LANES), jnp.float32),
            chunk(8), chunk(4), chunk(CHIPS, 4), chunk(8), chunk(16), chunk(8), chunk(CHIPS, 8), chunk(16),
            dma((3,)), dma((5,)), dma((NZ,)), dma((19,)),
        ],
        compiler_params=pltpu.CompilerParams(
            collective_id=0, has_side_effects=True, vmem_limit_bytes=VMEM_LIMIT
        ),
        name="collect",
    )(far(phases), far(slow_picks), far(mode_basis), far(tiled))
    near = lambda x: pltpu.with_memory_space_constraint(x, pltpu.VMEM)
    return pl.pallas_call(
        update,
        out_shape=jax.ShapeDtypeStruct((STEPS, POINTS), jnp.float32),
        in_specs=[vmem, vmem, vmem, vmem, hbm],
        out_specs=hbm,
        scratch_shapes=[
            pltpu.VMEM((STEPS, POINTS), jnp.float32),
            pltpu.VMEM((STEPS, POINTS), jnp.float32),
            pltpu.VMEM((2 * STEPS, 4 * M), jnp.bfloat16),
            pltpu.VMEM((3, R, 3 * LANES), jnp.float32),
            pltpu.VMEM((3, R, 3 * LANES), jnp.float32),
            pltpu.VMEM((STEPS, 4 * M), jnp.float32),
            pltpu.VMEM((4 * M, R), jnp.float32),
            dma(()), dma((POINTS // WIDTH,)),
        ],
        compiler_params=pltpu.CompilerParams(vmem_limit_bytes=VMEM_LIMIT),
        name="update",
    )(near(sums), near(chosen), near(among), near(rows), far(record))


def solution(mesh):
    in_specs = (P("tm", "space"), P(), P(), P())
    return jax.shard_map(body, mesh=mesh, in_specs=in_specs, out_specs=P("tm", "space"), check_vma=False)
```

```python
import jax
import jax.numpy as jnp
from jax import lax
from jax.experimental import pallas as pl
from jax.experimental.pallas import tpu as pltpu
from jax.sharding import PartitionSpec as P

M = 48
R = 32
LANES = 128
WIDTH = 512
EPS = 1e-5
AHEAD = 4
MESH = pl.DeviceIdType.MESH
EXACT = lax.Precision.HIGHEST
VMEM_LIMIT = 24 * 1024 * 1024
NT = 16
NS = 16
NZ = NT // 2
CHIPS = NS // 2
GROUP = 4
STEPS = 192
POINTS = 4096
SEGS = POINTS // LANES
TILES = STEPS // 8
BLOCK = SEGS * 8
ROWS0 = M // NT
ROWS1 = M // GROUP
X0 = STEPS
X1 = X0 + M
X2 = X1 + M
ALL = X2 + 2 * M
LANE1 = 64
LANE0 = 96


def dot_nt(a, b):
    return lax.dot_general(a, b, (((1,), (1,)), ((), ())), preferred_element_type=jnp.float32)


def exact(a, b, dims=((1,), (0,))):
    return lax.dot_general(a, b, (dims, ((), ())), precision=EXACT, preferred_element_type=jnp.float32)


def collect(
    phases_hbm, picks_hbm, basis_hbm, record,
    rows, sums, chosen, among,
    phases, picks, head, field_even, field_odd, got0, got1, wide0, wide1, basis, turned, pad,
    part2, inbox2, halves2, total2, part01, inbox01, halves01, total01,
    load_sem, small_sem, recv0_sem, sem,
):
    send0_sem, sendy_sem, recvy_sem, send1_sem, recv1_sem = [sem.at[i] for i in range(5)]
    sems2, sems01 = [[sem.at[i] for i in range(j, j + 6)] for j in (5, 11)]
    recvp_sem, late_sem = sem.at[17], sem.at[18]
    me_t = lax.axis_index("tm")
    me_s = lax.axis_index("space")
    core = lax.rem(me_s, 2)
    first = me_t // GROUP * GROUP

    barrier = pltpu.get_barrier_semaphore()
    for d in range(2, NT, 2):
        pl.semaphore_signal(barrier, inc=1, device_id={"tm": lax.rem(me_t + d, NT)}, device_id_type=MESH)
    partner = me_t + 1 - 2 * lax.rem(me_t, 2)
    pl.semaphore_signal(barrier, inc=1, device_id={"tm": partner}, device_id_type=MESH)
    chip = me_s // 2
    mate = me_s + 1 - 2 * core
    for d in range(1, CHIPS):
        peer = 2 * lax.rem(chip + d, CHIPS) + core
        pl.semaphore_signal(barrier, inc=1, device_id={"space": peer}, device_id_type=MESH)
    pl.semaphore_signal(barrier, inc=1, device_id={"space": mate}, device_id_type=MESH)

    get_phases = pltpu.make_async_copy(phases_hbm, phases, small_sem.at[3])
    get_phases.start()
    load_even, load_odd = [
        pltpu.make_async_copy(record.at[:, :, i], half.reshape(ROWS0 + 1, ROWS1 // ROWS0, BLOCK, LANES).at[pl.ds(0, ROWS0)], load_sem.at[i])
        for i, half in enumerate((field_even, field_odd))
    ]
    load_head = pltpu.make_async_copy(record.at[:, 0, 0], head.reshape(ROWS0, BLOCK, LANES), load_sem.at[2])
    load_head.start()
    load_even.start()
    q1 = 1 + me_t // GROUP
    q2 = 5 + me_t
    fetches = [
        pltpu.make_async_copy(basis_hbm.at[q], basis.at[level], small_sem.at[level])
        for level, q in enumerate((0, q1, q2))
    ]
    fetches.append(pltpu.make_async_copy(picks_hbm, picks, small_sem.at[4]))
    for fetch in fetches:
        fetch.start()
    load_odd.start()

    get_phases.wait()
    off0 = lax.rem(phases[0], STEPS * NT // M)
    off1 = lax.rem(phases[q1], STEPS * GROUP // M)
    off2 = lax.rem(phases[q2], STEPS // M)
    load_head.wait()
    for r in range(ROWS0):
        got0[me_t, r * SEGS : (r + 1) * SEGS] = head[pl.ds(r * BLOCK + off0, SEGS, stride=8), :].astype(jnp.bfloat16)

    pl.semaphore_wait(barrier, NZ + CHIPS)

    z = me_t // 2
    h = lax.rem(me_t, 2)
    near = me_t + 2 - 4 * lax.rem(z, 2)
    across = near + 1 - 2 * h

    def along0(target, owner, send_sem, recv_sem):
        return pltpu.make_async_remote_copy(
            src_ref=got0.at[owner], dst_ref=got0.at[owner], send_sem=send_sem, recv_sem=recv_sem,
            device_id={"tm": target}, device_id_type=MESH,
        )

    def along1(target, owner, recv_sem):
        return pltpu.make_async_remote_copy(
            src_ref=got1.at[owner - first], dst_ref=got1.at[owner - first],
            send_sem=send1_sem, recv_sem=recv_sem,
            device_id={"tm": target}, device_id_type=MESH,
        )

    def whole(ref, count, send_sem, recv_sem):
        place = ref.at[pl.ds(0, count)]
        return pltpu.make_async_remote_copy(
            src_ref=place, dst_ref=place, send_sem=send_sem, recv_sem=recv_sem,
            device_id={"tm": partner}, device_id_type=MESH,
        )

    hops = (1, -1, 2, -2, 3, -3, 4)
    turn = [lax.rem(z + d + NZ, NZ) for d in hops]
    out0 = [along0(2 * turn[i] + h, me_t, send0_sem, recv0_sem.at[z]) for i in range(7)]
    in0 = [along0(2 * turn[i] + h, 2 * turn[i] + h, send0_sem, recv0_sem.at[turn[i]]) for i in range(7)]
    over0 = [along0(partner, 2 * turn[i] + h, sendy_sem, recvy_sem if i < 4 else late_sem) for i in range(7)]
    over0.append(along0(partner, me_t, sendy_sem, recvy_sem))
    peers1 = (near, partner, across)
    out1 = [along1(near, me_t, recv1_sem), along1(partner, me_t, recvp_sem), along1(near, partner, recv1_sem)]
    in_partner = along1(partner, partner, recvp_sem)
    for copy in (over0[7], *out0):
        copy.start()
    load_even.wait()
    for r in range(ROWS1):
        got1[me_t - first, r * SEGS : (r + 1) * SEGS] = field_even[
            pl.ds(r * BLOCK + off1, SEGS, stride=8), :
        ].astype(jnp.bfloat16)
    out1[1].start()

    def widen(wide, got, slot):
        count = got.shape[1] // SEGS
        for r in range(count):
            wide[pl.ds(slot * count + r, SEGS, stride=M), :] = got[slot, r * SEGS : (r + 1) * SEGS].astype(jnp.float32)

    def pass0(i):
        in0[i].wait_recv()
        over0[i].start()
        widen(wide0, got0, 2 * turn[i] + h)

    load_odd.wait()

    def part_columns(c, carry):
        cols = pl.ds(pl.multiple_of(c * LANES, LANES), LANES)
        at = pl.multiple_of(c * 8, 8)
        for p in range(TILES // 2):
            pair = jnp.concatenate(
                [field_even[pl.ds(p * BLOCK + at, 8), :], field_odd[pl.ds(p * BLOCK + at, 8), :]], axis=0
            )
            rows[16 * p : 16 * (p + 1), cols] = pair.astype(jnp.bfloat16)
        x2 = jnp.concatenate(
            [
                half[pl.ds(at + off2 + more, TILES // 2, stride=BLOCK), :]
                for half in (field_even, field_odd)
                for more in (0, 4)
            ],
            axis=0,
        )
        high2 = x2.astype(jnp.bfloat16)
        rows[X2 : X2 + M, cols] = high2
        rows[X2 + M :, cols] = (x2 - high2.astype(jnp.float32)).astype(jnp.bfloat16)
        return carry

    lax.fori_loop(0, SEGS, part_columns, 0)
    widen(wide0, got0, me_t)
    widen(wide1, got1, me_t - first)

    for fetch in fetches:
        fetch.wait()
    none = lambda count: [jnp.full((1, R), -1, jnp.int32)] * count
    row_m = lax.broadcasted_iota(jnp.int32, (M, LANES), 0)
    for level, (q, place, at) in enumerate(((0, 3, 0), (q1, 2, M), (q2, 0, 2 * M))):
        spots = jnp.concatenate([*none(place), picks[pl.ds(q, 1), :], *none(3 - place)], axis=1)
        columns = exact(basis[level], (row_m == spots).astype(jnp.float32))
        if level == 2:
            pad[:M] = columns
            columns = jnp.concatenate([pad[pl.ds(i, M // 4, stride=4), :] for i in range(4)], axis=0)
            chosen[3 * M :] = columns
        chosen[at : at + M] = columns
    turned[...] = chosen[...].T
    at_row = lax.broadcasted_iota(jnp.int32, (STEPS, M), 0)
    order = lax.broadcasted_iota(jnp.int32, (STEPS, M), 1)
    rank = lax.rem(order, M // 4) * 4 + order // (M // 4)
    among[...] = exact((at_row == 4 * rank + off2).astype(jnp.float32), chosen[2 * M : 3 * M])
    def put(ref, tiles):
        for g in range(tiles[0].shape[0] // 8):
            for t in range(2):
                ref[2 * g + t] = tiles[t][8 * g : 8 * (g + 1)]

    space = jnp.zeros((R, 2 * LANES - STEPS), jnp.float32)
    by_field2 = exact(turned[:R, 2 * M :], dot_nt(rows[:STEPS], rows[X2:]), ((1,), (1,)))
    put(part2, [by_field2[:, :LANES], jnp.concatenate([by_field2[:, LANES:], space], axis=1)])

    def to_mate(src, dst, sems):
        return pltpu.make_async_remote_copy(
            src_ref=src, dst_ref=dst, send_sem=sems[0], recv_sem=sems[1],
            device_id={"space": mate}, device_id_type=MESH,
        )

    class Sum:
        def __init__(self, part, inbox, halves, total, sems):
            self.part, self.inbox, self.halves, self.total, self.sems = part, inbox, halves, total, sems
            count = inbox.shape[0]
            self.mine = pl.ds(core * count, count)
            self.give = to_mate(part.at[pl.ds(count - core * count, count)], inbox, sems[:2])
            self.back = to_mate(total.at[self.mine], total.at[self.mine], sems[4:])

        def swap(self):
            self.give.wait_recv()
            self.halves[chip] = self.part[self.mine] + self.inbox[...]
            for d in range(1, CHIPS):
                pltpu.make_async_remote_copy(
                    src_ref=self.halves.at[chip], dst_ref=self.halves.at[chip],
                    send_sem=self.sems[2], recv_sem=self.sems[3],
                    device_id={"space": 2 * lax.rem(chip + d, CHIPS) + core}, device_id_type=MESH,
                ).start()

        def add(self):
            self.swapped().wait_recv()
            acc = self.halves[0]
            for i in range(1, CHIPS):
                acc = acc + self.halves[i]
            self.total[self.mine] = acc
            self.back.start()

        def swapped(self):
            return whole(self.halves, CHIPS - 1, self.sems[2], self.sems[3])

        def settle(self):
            self.give.wait_send()
            self.swapped().wait_send()
            self.back.wait_send()

    sum2 = Sum(part2, inbox2, halves2, total2, sems2)
    sum01 = Sum(part01, inbox01, halves01, total01, sems01)
    sum2.give.start()

    for i in range(7):
        pass0(i)
        if i == 1:
            out1[0].start()
        if i == 3:
            in_partner.wait_recv()
            out1[2].start()

    sum2.swap()

    def unpack(wide, at):
        for j in range(SEGS):
            rows[at : at + M, j * LANES : (j + 1) * LANES] = wide[j * M : (j + 1) * M].astype(jnp.bfloat16)

    whole(got1, 2, send1_sem, recv1_sem).wait_recv()
    for peer in peers1:
        widen(wide1, got1, peer - first)
    unpack(wide1, X1)
    whole(got0, 5, sendy_sem, recvy_sem).wait_recv()
    for zz in (*turn[:4], z):
        widen(wide0, got0, 2 * zz + 1 - h)
    whole(got0, 3, sendy_sem, late_sem).wait_recv()
    for zz in turn[4:]:
        widen(wide0, got0, 2 * zz + 1 - h)
    unpack(wide0, X0)

    samples = rows[X0:X2]
    by_field = dot_nt(samples, rows[:STEPS])
    by_modes = exact(dot_nt(samples, samples), chosen[: 2 * M])
    ends = jnp.concatenate([by_field[:, LANES:], by_modes[:, LANE1:]], axis=1)
    both = exact(turned[LANE1:, : 2 * M], jnp.concatenate([by_field[:, :LANES], ends], axis=1))
    put(part01, [both[:, :LANES], both[:, LANES:]])

    sum01.give.start()
    sum01.swap()
    sum2.add()
    sum01.add()
    sum2.back.wait_recv()
    sums[16:] = total2[...]
    sum01.back.wait_recv()
    sums[:16] = total01[...]

    whole(got0, NZ - 1, send0_sem, recv0_sem.at[z]).wait_send()
    whole(got0, NZ, sendy_sem, recvy_sem).wait_send()
    whole(got1, GROUP - 1, send1_sem, recv1_sem).wait_send()
    sum2.settle()
    sum01.settle()


def eliminate(tiles, pivot_tile, pivot_lane):
    sub = lax.broadcasted_iota(jnp.int32, (8, LANES), 0)
    over = lambda x, i: jnp.broadcast_to(x[i : i + 1], (8, LANES))
    count = len(tiles[0])
    ahead = {}
    for k in range(0, R, 2):
        g, i = divmod(k, 8)
        for j in range(k, min(k + 2 * AHEAD + 2, R)):
            if j not in ahead:
                lane = pivot_lane + j
                ahead[j] = [jnp.broadcast_to(row[pivot_tile][:, lane : lane + 1], (8, LANES)) for row in tiles]
        left, right = ahead.pop(k), ahead.pop(k + 1)
        a, b, c, d = over(left[g], i), over(right[g], i), over(left[g], i + 1), over(right[g], i + 1)
        scale = 1.0 / (a * d - b * c)
        a, b, c, d = a * scale, b * scale, c * scale, d * scale

        def pivot(old):
            first, second = over(old[g], i), over(old[g], i + 1)
            upper, lower = d * first - b * second, a * second - c * first
            moved = [old[q] - (left[q] * upper + right[q] * lower) for q in range(len(old))]
            moved[g] = jnp.where(sub == i, upper, jnp.where(sub == i + 1, lower, moved[g]))
            return moved

        ahead = {j: pivot(old) for j, old in ahead.items()}
        columns = [pivot([row[t] for row in tiles]) for t in range(count)]
        tiles = [[columns[t][q] for t in range(count)] for q in range(R // 8)]
    return tiles


def solve(block, pivot):
    tile, at = divmod(pivot, LANES)
    sub = lax.broadcasted_iota(jnp.int32, (8, LANES), 0)
    lane = lax.broadcasted_iota(jnp.int32, (8, LANES), 1)
    tiles = [
        [block[8 * g : 8 * (g + 1), LANES * t : LANES * (t + 1)] for t in range(block.shape[1] // LANES)]
        for g in range(R // 8)
    ]
    for g in range(R // 8):
        tiles[g][tile] = jnp.where(lane == at + 8 * g + sub, tiles[g][tile] + EPS, tiles[g][tile])
    done = eliminate(tiles, tile, at)
    return jnp.concatenate([jnp.concatenate(row, axis=1) for row in done], axis=0)


def update(sums, chosen, among, rows, record, out_hbm, field, out, weights, held, done, early, last, load_sem, store_sem):
    live = lax.axis_index("tm") >= 0
    at1, at0, at2 = LANES + LANE1, LANES + LANE0, 2 * LANES

    load = pltpu.make_async_copy(record, field, load_sem)
    load.start()
    @pl.when(live)
    def _():
        scale = 1.0 / (POINTS * NS)
        tall = lambda first, t: jnp.concatenate([sums[first + 2 * g + t] for g in range(R // 8)], axis=0) * scale
        blocks = []
        for first in (8, 0, 16):
            left, right = tall(first, 0), tall(first, 1)
            by_field = jnp.concatenate([left, right], axis=1)[:, :STEPS]
            blocks.append(jnp.concatenate([left, right, exact(by_field, among[...])], axis=1))
        for level in range(3):
            held[level] = blocks[level]
        done[0] = solve(blocks[0], at0)

    def change(block, done, at):
        cols = slice(at, at + R)
        return exact(block[:, cols] + EPS * done[:, cols], done, ((0,), (0,)))

    @pl.when(live)
    def _():
        held[1] = held[1] - change(held[0], done[0], at1)

    @pl.when(live)
    def _():
        held[2] = held[2] - change(held[0], done[0], at2)
        pick0 = chosen[:M, LANE0 : LANE0 + R]
        done0 = done[0]
        way1 = -exact(pick0, done0[:, at1 : at1 + R])
        last[M : 2 * M] = way1
        last[:M] = -exact(pick0, done0[:, at2 : at2 + R])
        early[:, :M] = exact(done0[:, :STEPS], pick0, ((0,), (1,)))
        early[:, 2 * M :] = jnp.zeros((STEPS, 2 * M), jnp.float32)
        done[1] = solve(held[1], at1)

    @pl.when(live)
    def _():
        held[2] = held[2] - change(held[1], done[1], at2)

    @pl.when(live)
    def _():
        pick1 = chosen[M : 2 * M, LANE1 : LANE1 + R]
        done1 = done[1]
        way1 = last[M : 2 * M]
        by_field1 = done1[:, :STEPS]
        early[:, :M] = early[:, :M] + exact(by_field1, way1, ((0,), (1,)))
        early[:, M : 2 * M] = exact(by_field1, pick1, ((0,), (1,)))
        last[:M] = last[:M] - exact(way1, done1[:, at2 : at2 + R])
        last[M : 2 * M] = -exact(pick1, done1[:, at2 : at2 + R])
        last[2 * M :] = chosen[2 * M :, :R]
        done[2] = solve(held[2], at2)

    @pl.when(live)
    def _():
        slopes = early[...] + exact(done[2][:, :STEPS], last[...], ((0,), (1,)))
        high = slopes.astype(jnp.bfloat16)
        weights[:STEPS] = high
        weights[STEPS:] = (slopes - high.astype(jnp.float32)).astype(jnp.bfloat16)

    load.wait()
    stores = []
    for c in range(POINTS // WIDTH):
        cols = slice(c * WIDTH, (c + 1) * WIDTH)
        slow = jnp.dot(weights[...], rows[X0:, cols], preferred_element_type=jnp.float32)
        out[:, cols] = field[:, cols] - (slow[:STEPS] + slow[STEPS:])
        store = pltpu.make_async_copy(out.at[:, cols], out_hbm.at[:, cols], store_sem.at[c])
        store.start()
        stores.append(store)
    for store in stores:
        store.wait()


def body(record, mode_basis, slow_picks, phases):
    dma = pltpu.SemaphoreType.DMA
    vmem = pl.BlockSpec(memory_space=pltpu.VMEM)
    hbm = pl.BlockSpec(memory_space=pltpu.MemorySpace.HBM)
    tiled = record.reshape(TILES, 8, SEGS, LANES).transpose(0, 2, 1, 3).reshape(ROWS0, ROWS1 // ROWS0, 2, BLOCK, LANES)
    far = lambda x: pltpu.with_memory_space_constraint(x, pltpu.MemorySpace.HBM)
    chunk = lambda *count: pltpu.VMEM((*count, 8, LANES), jnp.float32)
    rows, sums, chosen, among = pl.pallas_call(
        collect,
        out_shape=[
            pltpu.VMEM((ALL, POINTS), jnp.bfloat16),
            pltpu.VMEM((24, 8, LANES), jnp.float32),
            pltpu.VMEM((4 * M, LANES), jnp.float32),
            pltpu.VMEM((STEPS, LANES), jnp.float32),
        ],
        in_specs=[hbm] * 4,
        out_specs=[vmem] * 4,
        scratch_shapes=[
            pltpu.SMEM((21,), jnp.int32),
            pltpu.VMEM((21, R), jnp.int32),
            pltpu.VMEM((ROWS0 * BLOCK, LANES), jnp.float32),
            pltpu.VMEM(((ROWS1 + ROWS1 // ROWS0) * BLOCK, LANES), jnp.float32),
            pltpu.VMEM(((ROWS1 + ROWS1 // ROWS0) * BLOCK, LANES), jnp.float32),
            pltpu.VMEM((NT, ROWS0 * SEGS, LANES), jnp.bfloat16),
            pltpu.VMEM((GROUP, ROWS1 * SEGS, LANES), jnp.bfloat16),
            pltpu.VMEM((M * SEGS, LANES), jnp.float32),
            pltpu.VMEM((M * SEGS, LANES), jnp.float32),
            pltpu.VMEM((3, M, M), jnp.float32),
            pltpu.VMEM((LANES, 4 * M), jnp.float32),
            pltpu.VMEM((M + 16, LANES), jnp.float32),
            chunk(8), chunk(4), chunk(CHIPS, 4), chunk(8), chunk(16), chunk(8), chunk(CHIPS, 8), chunk(16),
            dma((3,)), dma((5,)), dma((NZ,)), dma((19,)),
        ],
        compiler_params=pltpu.CompilerParams(
            collective_id=0, has_side_effects=True, vmem_limit_bytes=VMEM_LIMIT
        ),
        name="collect",
    )(far(phases), far(slow_picks), far(mode_basis), far(tiled))
    near = lambda x: pltpu.with_memory_space_constraint(x, pltpu.VMEM)
    return pl.pallas_call(
        update,
        out_shape=jax.ShapeDtypeStruct((STEPS, POINTS), jnp.float32),
        in_specs=[vmem, vmem, vmem, vmem, hbm],
        out_specs=hbm,
        scratch_shapes=[
            pltpu.VMEM((STEPS, POINTS), jnp.float32),
            pltpu.VMEM((STEPS, POINTS), jnp.float32),
            pltpu.VMEM((2 * STEPS, 4 * M), jnp.bfloat16),
            pltpu.VMEM((3, R, 3 * LANES), jnp.float32),
            pltpu.VMEM((3, R, 3 * LANES), jnp.float32),
            pltpu.VMEM((STEPS, 4 * M), jnp.float32),
            pltpu.VMEM((4 * M, R), jnp.float32),
            dma(()), dma((POINTS // WIDTH,)),
        ],
        compiler_params=pltpu.CompilerParams(vmem_limit_bytes=VMEM_LIMIT),
        name="update",
    )(near(sums), near(chosen), near(among), near(rows), far(record))


def solution(mesh):
    in_specs = (P("tm", "space"), P(), P(), P())
    return jax.shard_map(body, mesh=mesh, in_specs=in_specs, out_specs=P("tm", "space"), check_vma=False)
```
